32 devices in a mesh: seg: 16 (over z, y, x), sub: 2 (over core).
Axes of the slice: x: 2, y: 2, z: 4, core: 2. Of those that a mesh axis runs over, the one named last changes fastest.
Arguments:
- near_blocks: bfloat16 [64, 10, 256, 256], P(('seg', 'sub')), may hold values from -0.375 to 0.375
- sample_cols: bfloat16 [16384, 256], P(('seg', 'sub')), may hold values from -6 to 6
- near_list: int32 [64, 10], P(('seg', 'sub')), may hold values from -1 to 63, as said below
- row_basis_t: bfloat16 [64, 64, 256], P(('seg', 'sub')), may hold values from -0.75 to 0.75
- col_basis_t: bfloat16 [64, 64, 256], P(('seg', 'sub')), may hold values from -0.375 to 0.375
- couplings: bfloat16 [16, 2, 16, 64, 128], P('seg', 'sub'), may hold values from -0.25 to 0.25
- far_source: int32 [16, 2, 16, 2], P('seg', 'sub'), may hold values from 0 to 2
- far_dest: int32 [16, 2, 16, 2], P('seg', 'sub'), may hold values from 0 to 1
Outputs:
- samples: bfloat16 [16384, 256], P(('seg', 'sub'))
- segment_factor: float32 [4096, 256], P('seg')
- transfers: bfloat16 [16, 3, 256, 256], P('seg')
The draws below stay inside these ranges and needn't reach their ends.
Inputs may be any that keep to these rules, and one draw needn't show every extreme that they name: `near_list`: entry 0 of every list is the leaf itself; -1 marks padding and stands only after the real entries; every other entry names a leaf held by the same device or by the device just before or just after it in the order of seg, then sub. `far_source`: entry [s', u, s, c] is the local leaf of device (s', u) whose far projection fills slot c toward device (s, u); the value 2 marks an empty slot. `far_dest`: entry [s, u, s', c] is the local leaf of device (s, u) that slot c from device (s', u) serves.
All inputs are finite; a program needn't handle non-finite values.
Results may differ from the reference program's by a relative error of at most 0.013.
Values may be sent and summed in bfloat16 or wider, within the bound.
No kernel may reach another device: no remote copies, remote signals or barrier semaphores. Data moves between devices by JAX's collectives and lax.ppermute only.
A program may use at most 64 MiB of HBM per device.

```python
import jax
import jax.numpy as jnp
from jax import lax

LEAF = 256
SAMP = 256
RANK = 64
NEAR = 10
CAP = 2
LEVELS = 3
LEAF_DEV = 2
LEAVES = 64
FAR_SLOTS = 32
N_SEG = 16
N_SUB = 2
DEVICES = 32


def draw_near_list(key, part):
    leaf_ids = jnp.arange(LEAVES, dtype=jnp.int32)
    device_ids = leaf_ids // LEAF_DEV
    offsets = jax.random.randint(jax.random.fold_in(key, 11), (LEAVES, NEAR), 0, 3 * LEAF_DEV)
    candidate = (device_ids[:, None] - 1) * LEAF_DEV + offsets
    in_range = (candidate >= 0) & (candidate < LEAVES)
    candidate = jnp.where(in_range, candidate, leaf_ids[:, None])
    list_length = jax.random.randint(jax.random.fold_in(key, 12), (LEAVES,), NEAR // 2 + 1, NEAR + 1)
    list_length = jnp.where(leaf_ids == 0, NEAR - 1, list_length)
    slot_ids = jnp.arange(NEAR, dtype=jnp.int32)[None, :]
    candidate = jnp.where(slot_ids == 0, leaf_ids[:, None], candidate)
    return jnp.where(slot_ids < list_length[:, None], candidate, -1).astype(jnp.int32)


def place_ends(array, key, low, largest):
    index_at = [jax.random.randint(jax.random.fold_in(key, axis), (), 0, length) for axis, length in enumerate(array.shape)]
    longest = array.shape.index(max(array.shape))
    neighbour = index_at[:longest] + [(index_at[longest] + 1) % array.shape[longest]] + index_at[longest + 1:]
    return array.at[tuple(index_at)].set(low).at[tuple(neighbour)].set(largest)


def block_scale(key, dims, cuts, low, high):
    factor_of, own = 1.0, jax.random.fold_in(key, 6)
    for axis_at, shards_of in cuts:
        draws = jnp.exp(jax.random.uniform(jax.random.fold_in(own, axis_at), (shards_of,), jnp.float32, low / len(cuts), high / len(cuts)))
        factor_of = factor_of * jnp.repeat(draws, dims[axis_at] // shards_of).reshape([-1 if axis == axis_at else 1 for axis in range(len(dims))])
    return factor_of


def noise(stream_key, shape, width, limit, pieces=(), held_as=jnp.bfloat16):
    array = width * jax.random.normal(stream_key, shape, jnp.float32)
    if pieces:
        array = array * block_scale(stream_key, shape, pieces, -0.22, 0.18)
    return jnp.clip(array, -limit, limit).astype(held_as)


def setup_inputs(seed: int = 0) -> dict:
    streams_of = jax.random.split(jax.random.key(seed), 9)
    return {
        "near_blocks": noise(streams_of[0], (LEAVES, NEAR, LEAF, LEAF), LEAF ** -0.5, 0.375, ((0, 32),)),
        "sample_cols": noise(streams_of[1], (LEAVES * LEAF, SAMP), 1.0, 6.0, ((0, 32),)),
        "near_list": draw_near_list(jax.random.fold_in(streams_of[8], 71), 0),
        "row_basis_t": noise(streams_of[3], (LEAVES, RANK, LEAF), RANK ** -0.5, 0.75, ((0, 32),)),
        "col_basis_t": noise(streams_of[4], (LEAVES, RANK, LEAF), LEAF ** -0.5, 0.375, ((0, 32),)),
        "couplings": noise(streams_of[5], (N_SEG, N_SUB, N_SEG, RANK, CAP * RANK), (RANK * FAR_SLOTS // 4) ** -0.5, 0.25, ((0, 16), (1, 2))),
        "far_source": place_ends(jax.random.randint(streams_of[6], (N_SEG, N_SUB, N_SEG, CAP), 0, LEAF_DEV + 1), jax.random.fold_in(streams_of[6], 1), 0, LEAF_DEV).astype(jnp.int32),
        "far_dest": place_ends(jax.random.randint(streams_of[7], (N_SEG, N_SUB, N_SEG, CAP), 0, LEAF_DEV), jax.random.fold_in(streams_of[7], 1), 0, LEAF_DEV - 1).astype(jnp.int32),
    }


def leaf_adjacent(block_set, index_collection, random_cols):
    usable = index_collection >= 0
    chosen = random_cols[jnp.where(usable, index_collection, 0)]
    chosen = jnp.where(usable[:, None, None], chosen, jnp.zeros_like(chosen))
    return jnp.einsum('kab,kbs->as', block_set.astype(jnp.float32), chosen.astype(jnp.float32), precision=lax.Precision.HIGHEST)

def reference(near_blocks, sample_cols, near_list, row_basis_t, col_basis_t, couplings, far_source, far_dest):
    random_cols = sample_cols.reshape(LEAVES, LEAF, SAMP)
    basis_projector = jnp.einsum('jra,jas->jrs', col_basis_t.astype(jnp.float32), random_cols.astype(jnp.float32), precision=lax.Precision.HIGHEST).astype(jnp.bfloat16)
    near_part = lax.map(lambda bundle: leaf_adjacent(bundle[0], bundle[1], random_cols), (near_blocks, near_list))
    source_t = jnp.transpose(far_source, (2, 1, 0, 3))
    owner_base = (jnp.arange(N_SEG, dtype=jnp.int32)[None, None, :, None] * N_SUB + jnp.arange(N_SUB, dtype=jnp.int32)[None, :, None, None]) * LEAF_DEV
    global_leaf = (owner_base + source_t).astype(jnp.int32).reshape(DEVICES, N_SEG, CAP)
    occupied = (source_t < LEAF_DEV).reshape(DEVICES, N_SEG, CAP)
    target_leaf = far_dest.reshape(DEVICES, N_SEG, CAP)
    coupling_set = couplings.reshape(DEVICES, N_SEG, RANK, CAP, RANK)

    def remote_processor(bundle):
        leaf_ids, alive, targets, coupling_one = bundle
        slot_data = basis_projector[jnp.where(alive, leaf_ids, 0)]
        slot_data = jnp.where(alive[:, :, None, None], slot_data, jnp.zeros_like(slot_data))
        routing = (targets[:, :, None] == jnp.arange(LEAF_DEV, dtype=jnp.int32)[None, None, :]).astype(jnp.float32)
        products = jnp.einsum('pacb,pcbs->pcas', coupling_one.astype(jnp.float32), slot_data.astype(jnp.float32), precision=lax.Precision.HIGHEST)
        return jnp.einsum('pcas,pcl->las', products, routing, precision=lax.Precision.HIGHEST)
    far_coeff = lax.map(remote_processor, (global_leaf, occupied, target_leaf, coupling_set)).astype(jnp.bfloat16)
    far_coeff = far_coeff.reshape(LEAVES, RANK, SAMP)
    distant_portion = jnp.einsum('jra,jrs->jas', row_basis_t.astype(jnp.float32), far_coeff.astype(jnp.float32), precision=lax.Precision.HIGHEST)
    samples = (near_part + distant_portion).astype(jnp.bfloat16).reshape(LEAVES * LEAF, SAMP)
    sample_rows = samples.reshape(DEVICES, LEAF_DEV * LEAF, SAMP).astype(jnp.float32)
    gram_local = jnp.einsum('dns,dnt->dst', sample_rows, sample_rows, precision=lax.Precision.HIGHEST)
    seg_gram = gram_local.reshape(N_SEG, N_SUB, SAMP, SAMP).sum(axis=1) / (N_SUB * LEAF_DEV * LEAF)
    gram_levels = [seg_gram]
    current = seg_gram
    for segment_position_index in range(LEVELS):
        paired = current.reshape(-1, 2, SAMP, SAMP)
        current = (paired[:, 0] + paired[:, 1]) * 0.5
        gram_levels.append(jnp.repeat(current, 2 ** (segment_position_index + 1), axis=0))
    stacked = jnp.stack(gram_levels, axis=1)
    triangles = jnp.linalg.cholesky(stacked)
    segment_factor = jnp.swapaxes(triangles[:, 0], 1, 2).reshape(N_SEG * SAMP, SAMP)
    solved = jax.vmap(jax.vmap(lambda upper_one, lower_one: jax.scipy.linalg.solve_triangular(upper_one, lower_one, lower=True)))(triangles[:, 1:], triangles[:, :-1])
    transfers = jnp.swapaxes(solved, 2, 3).astype(jnp.bfloat16)
    return (samples, segment_factor, transfers)
```

```python
import jax
import jax.numpy as jnp
from jax import lax
from jax.experimental import pallas as pl
from jax.experimental.pallas import tpu as pltpu
from jax.sharding import PartitionSpec as P

LEVELS = 3


def padded(value, sides, width):
    for axis, dim in sides:
        size, length = (lax.axis_size(axis), value.shape[dim])
        up = [(i, (i + 1) % size) for i in range(size - 1)]
        down = [(j, i) for i, j in up]
        last = lax.slice_in_dim(value, length - width, length, axis=dim)
        leading = lax.slice_in_dim(value, 0, width, axis=dim)
        before = lax.ppermute(last, axis, up)
        after = lax.ppermute(leading, axis, down)
        value = jnp.concatenate([before, value, after], axis=dim)
    return value


def from_partner(value, axis, distance):
    mask = 2**distance
    pairs = [(source, source ^ mask) for source in range(lax.axis_size(axis))]
    return lax.ppermute(value, axis, pairs)


def rb(x,k): return jnp.broadcast_to(x[k:k+1,:],(8,128))

def split(a):
    h=a.astype(jnp.bfloat16); return h,(a-h.astype(jnp.float32)).astype(jnp.bfloat16)
def dg(a,b,dims): return lax.dot_general(a,b,(dims,((),())),preferred_element_type=jnp.float32)
def mm3(a,b,dims):
    ah,al=split(a); bh,bl=split(b)
    return dg(ah,bh,dims)+dg(ah,bl,dims)+dg(al,bh,dims)
def mm(a,b): return mm3(a,b,((1,),(0,)))
def mmt(a,b): return mm3(a,b,((1,),(1,)))
def eliminate(P, lane, row):
    base=lane & ~31
    sub=lane & 31
    V=[jnp.where(row+8*rv==sub,1.0,0.0).astype(jnp.float32) for rv in range(4)]
    P=list(P)
    for m in range(4):
        C=[[jnp.take_along_axis(P[rv],base+(8*m+k),axis=1,mode="promise_in_bounds") for rv in range(m,4)] for k in range(8)]
        piv=jnp.ones((8,128),jnp.float32)
        for k in range(8):
            d=rb(C[k][0],k)
            piv=jnp.where(row==k,d,piv)
            inv=1.0/d
            M=[c*inv for c in C[k]]
            M[0]=jnp.where(row>k,M[0],0.0)
            for k2 in range(k+1,8):
                f=rb(C[k2][0],k)
                C[k2]=[c-mu*f for c,mu in zip(C[k2],M)]
            fp=rb(P[m],k); fv=rb(V[m],k)
            for rv in range(m,4):
                P[rv]=P[rv]-M[rv-m]*fp
                V[rv]=V[rv]-M[rv-m]*fv
        rs=lax.rsqrt(piv)
        P[m]=P[m]*rs
        V[m]=V[m]*rs
    return P,V

def factor_kernel(g_ref,r_ref,tr_ref,X,Rb,Wb):
    n=256
    lane=lax.broadcasted_iota(jnp.int32,(8,128),1); row=lax.broadcasted_iota(jnp.int32,(8,128),0)
    grp=lane//32
    l32=lax.broadcasted_iota(jnp.int32,(32,256),1)
    r32=lax.broadcasted_iota(jnp.int32,(32,256),0)
    bd=(lax.broadcasted_iota(jnp.int32,(128,128),0)//32)==(lax.broadcasted_iota(jnp.int32,(128,128),1)//32)
    l256=lax.broadcasted_iota(jnp.int32,(128,256),1); r256=lax.broadcasted_iota(jnp.int32,(128,256),0)&31
    for kb in range(8):
        for t in range(4):
            X[kb,32*t:32*t+32,:]=g_ref[t,32*kb:32*kb+32,:]
    for kb in range(8):
        off=32*kb; c0=off//128*128; lo=off%128
        P=[]
        for rv in range(4):
            acc=None
            for t in range(4):
                v=X[kb,t*32+8*rv:t*32+8*rv+8,c0:c0+128]
                sh=(32*t-lo)%128
                if sh: v=pltpu.roll(v,sh,1)
                acc=v if acc is None else jnp.where(grp==t,v,acc)
            P.append(acc)
        P,V=eliminate(P,lane,row)
        Pf=jnp.concatenate(P,0); Vf=jnp.concatenate(V,0)
        Wbd=jnp.where(bd,jnp.concatenate([Vf]*4,0),0.0)
        x=X[kb]
        x=jnp.where((l256>=off)&(l256<off+32),jnp.where(l256-off==r256,1.0,0.0),x)
        panel=mm(Wbd,x)
        chunks={}
        for i in range(kb+1,8):
            c=i//4
            if c not in chunks: chunks[c]=jnp.transpose(panel[:,c*128:c*128+128])
            T=chunks[c][(i%4)*32:(i%4)*32+32,:]
            L=jnp.where(bd,jnp.concatenate([T]*4,0),0.0)
            X[i]=jnp.where((l256>=off)&(l256<off+32),0.0,X[i])-mm(L,panel)
        for t in range(4):
            pt=panel[32*t:32*t+32,:]
            sh=(lo-32*t)%128
            d=Pf
            if sh: d=pltpu.roll(d,sh,1)
            d2=jnp.concatenate([d,d],1)
            Rb[t,off:off+32,:]=jnp.where(l32>=off+32,pt,jnp.where((l32>=off)&(l32-off>=r32),d2,0.0))
            if t>0: Wb[t-1,off:off+32,:]=jnp.where(l32<off+32,pt,0.0)
    r_ref[...]=Rb[0]
    for t in range(3):
        tr_ref[t]=mmt(Rb[t],Wb[t]).astype(jnp.bfloat16)

def factor_all(grams):
    return pl.pallas_call(
        factor_kernel,
        out_shape=(
            jax.ShapeDtypeStruct((256, 256), jnp.float32),
            jax.ShapeDtypeStruct((LEVELS, 256, 256), jnp.bfloat16),
        ),
        in_specs=[pl.BlockSpec(memory_space=pltpu.VMEM)],
        out_specs=[pl.BlockSpec(memory_space=pltpu.VMEM)] * 2,
        scratch_shapes=[
            pltpu.VMEM((8, 128, 256), jnp.float32),
            pltpu.VMEM((4, 256, 256), jnp.float32),
            pltpu.VMEM((3, 256, 256), jnp.float32),
        ],
        compiler_params=pltpu.CompilerParams(vmem_limit_bytes=32 * 2**20),
    )(grams)


def body(
    near_blocks, sample_cols, near_list, row_basis_t, col_basis_t, couplings, far_source, far_dest
):
    leaf_count, near_count, leaf_rows, _ = near_blocks.shape
    sample_width = sample_cols.shape[1]
    rank_width = row_basis_t.shape[1]
    seg_count = lax.axis_size("seg")
    slot_number_count = far_source.shape[3]
    random_cols = sample_cols.reshape(leaf_count, leaf_rows, sample_width)
    basis_projector = jnp.einsum(
        "jra,jas->jrs", col_basis_t, random_cols, preferred_element_type=jnp.float32
    ).astype(jnp.bfloat16)
    extended = padded(sample_cols, ((("seg", "sub"), 0),), leaf_count * leaf_rows)
    extended = extended.reshape(3 * leaf_count, leaf_rows, sample_width)
    base_leaf = (lax.axis_index(("seg", "sub")) - 1) * leaf_count
    usable = near_list >= 0
    position = jnp.where(usable, near_list - base_leaf, 0)
    chosen = extended[position]
    chosen = jnp.where(usable[:, :, None, None], chosen, jnp.zeros_like(chosen))
    near_part = jnp.einsum(
        "lkab,lkbs->las", near_blocks, chosen, preferred_element_type=jnp.float32
    )
    leaf_range = jnp.arange(leaf_count, dtype=jnp.int32)
    routing = far_dest[0, 0][:, :, None] == leaf_range[None, None, :]
    coupling_set = jnp.transpose(
        couplings[0, 0].reshape(seg_count, rank_width, slot_number_count, rank_width), (1, 0, 2, 3)
    )
    masked = jnp.where(
        jnp.transpose(routing, (2, 0, 1))[:, None, :, :, None],
        coupling_set[None],
        jnp.zeros((), jnp.bfloat16),
    )
    masked = masked.reshape(leaf_count * rank_width, seg_count * slot_number_count * rank_width)
    selection_choice = (far_source[0, 0][:, :, None] == leaf_range[None, None, :]).astype(
        jnp.bfloat16
    )
    outgoing = jnp.einsum(
        "zgy,ykf->zgkf", selection_choice, basis_projector, preferred_element_type=jnp.float32
    ).astype(jnp.bfloat16)
    incoming = lax.all_to_all(outgoing, "seg", split_axis=0, concat_axis=0, tiled=True)
    far_total = jnp.dot(
        masked,
        incoming.reshape(seg_count * slot_number_count * rank_width, sample_width),
        preferred_element_type=jnp.float32,
    )
    far_coeff = far_total.astype(jnp.bfloat16).reshape(leaf_count, rank_width, sample_width)
    distant_portion = jnp.einsum(
        "lra,lrs->las", row_basis_t, far_coeff, preferred_element_type=jnp.float32
    )
    samples = (
        (near_part + distant_portion)
        .astype(jnp.bfloat16)
        .reshape(leaf_count * leaf_rows, sample_width)
    )
    gram_local = lax.dot_general(
        samples, samples, (((0,), (0,)), ((), ())), preferred_element_type=jnp.float32
    )
    row_total = lax.axis_size("sub") * leaf_count * leaf_rows
    total, distance = gram_local, 0
    while 2**distance < lax.axis_size("sub"):
        rounded = total.astype(jnp.bfloat16)
        total = rounded.astype(jnp.float32) + from_partner(rounded, "sub", distance).astype(
            jnp.float32
        )
        distance += 1
    current = total / row_total
    gram_levels = [current]
    for segment_position_index in range(LEVELS):
        partner = from_partner(current.astype(jnp.bfloat16), "seg", segment_position_index).astype(
            current.dtype
        )
        current = (current + partner) * 0.5
        gram_levels.append(current)
    stacked = jnp.stack(gram_levels)
    segment_factor, transfers = factor_all(stacked)
    return (samples, segment_factor, transfers[None])


def solution(mesh):
    in_specs = (
        P(("seg", "sub"), None, None, None),
        P(("seg", "sub"), None),
        P(("seg", "sub"), None),
        P(("seg", "sub"), None, None),
        P(("seg", "sub"), None, None),
        P("seg", "sub", None, None, None),
        P("seg", "sub", None, None),
        P("seg", "sub", None, None),
    )
    out_specs = (P(("seg", "sub"), None), P("seg", None), P("seg", None, None, None))
    return jax.shard_map(body, mesh=mesh, in_specs=in_specs, out_specs=out_specs, check_vma=False)
```

```python
import jax
import jax.numpy as jnp
from jax import lax
from jax.experimental import pallas as pl
from jax.experimental.pallas import tpu as pltpu
from jax.sharding import PartitionSpec as P

LEVELS = 3
AXES = ("seg", "sub")
VMEM = pl.BlockSpec(memory_space=pltpu.VMEM)
SMEM = pl.BlockSpec(memory_space=pltpu.SMEM)


def params(**more):
    return pltpu.CompilerParams(vmem_limit_bytes=48 * 2**20, **more)


def hop(value, even, odd):
    n_seg, n_sub = lax.axis_size("seg"), lax.axis_size("sub")
    pairs = []
    for s in range(n_seg):
        for u in range(n_sub):
            mask = odd if u % 2 else even
            if mask:
                pairs.append((s * n_sub + u, (s ^ mask) * n_sub + u))
    return lax.ppermute(value, AXES, pairs)


def sub_hop(value, mask):
    return lax.ppermute(value, "sub", [(i, i ^ mask) for i in range(lax.axis_size("sub"))])


def pack(top, low):
    lane = lax.broadcasted_iota(jnp.int32, (64, 128), 1)
    corner = pltpu.roll(low[64:128, :], 64, 1)
    mixed = jnp.where(lane < 64, corner, top[64:128, 0:128])
    return jnp.concatenate([top[0:64, 0:128], mixed, top[:, 128:256], low[0:64, :]], 0)


def unpack(packed):
    zero = jnp.zeros((64, 128), jnp.float32)
    left = jnp.concatenate([packed[0:128, :], zero, zero], 0)
    right = jnp.concatenate(
        [packed[128:256, :], packed[256:320, :], pltpu.roll(packed[64:128, :], 64, 1)], 0
    )
    return jnp.concatenate([left, right], 1)


def dot(a, b):
    return jnp.dot(a, b, preferred_element_type=jnp.float32)


def dot_t(a, b):
    return lax.dot_general(a, b, (((0,), (0,)), ((), ())), preferred_element_type=jnp.float32)


def project_kernel(basis_ref, cols_ref, source_ref, out_ref):
    leaves, rank, rows = basis_ref.shape
    lane = lax.broadcasted_iota(jnp.int32, (8, 256), 1)
    flags = jnp.zeros((8, 256), jnp.float32)
    for s in range(source_ref.shape[0]):
        for c in range(source_ref.shape[1]):
            flags = jnp.where(
                lane == s * source_ref.shape[1] + c, source_ref[s, c].astype(jnp.float32), flags
            )
    for l in range(leaves):
        out_ref[0, l * rank : (l + 1) * rank, :] = dot(
            basis_ref[l], cols_ref[l * rows : (l + 1) * rows, :]
        ).astype(jnp.bfloat16)
    out_ref[0, leaves * rank : leaves * rank + 8, :] = flags.astype(jnp.bfloat16)


def near_kernel(list_ref, blocks_ref, own_ref, swap_ref, cross_ref, out_ref, held):
    leaf = pl.program_id(0)
    leaves = held.shape[0] // 3

    @pl.when(leaf == 0)
    def _():
        for j in range(leaves):
            rows = slice(j * 256, (j + 1) * 256)
            held[j] = own_ref[rows, :]
            held[leaves + j] = swap_ref[rows, :]
            held[2 * leaves + j] = cross_ref[rows, :]
        held[3 * leaves] = jnp.zeros_like(held[0])

    device = lax.axis_index("seg") * lax.axis_size("sub") + lax.axis_index("sub")
    odd = device % 2
    before = (2 - odd) * leaves
    after = (1 + odd) * leaves
    acc = jnp.zeros((256, 256), jnp.float32)
    for k in range(blocks_ref.shape[1]):
        entry = list_ref[leaf, k]
        shift = entry - device * leaves
        slot = jnp.where(
            shift < 0, before + leaves + shift, jnp.where(shift < leaves, shift, after + shift - leaves)
        )
        slot = jnp.where(entry < 0, 3 * leaves, slot)
        acc = acc + dot(blocks_ref[0, k], held[slot])
    out_ref[...] = acc


def combine_kernel(dest_ref, couplings_ref, basis_ref, near_ref, *refs):
    b_ref, q1, q2, q3, z_ref, r1, r2, r3, samples_ref, gram_ref = refs
    me = lax.axis_index("seg")
    leaves, rank, rows = basis_ref.shape
    slots = dest_ref.shape[1]
    blocks = [(b_ref, 0, 0), (q1, 0, 1), (q2, 0, 2), (q3, 0, 3)]
    for mask, ref in ((0, z_ref), (1, r1), (2, r2), (3, r3)):
        blocks += [(ref, k, mask ^ (4 * k + 4)) for k in range(ref.shape[0])]
    lane8 = lax.broadcasted_iota(jnp.int32, (8, 256), 1)
    lane = lax.broadcasted_iota(jnp.int32, (1, slots * rank), 1)
    total = jnp.zeros((leaves * rank, 256), jnp.float32)
    for ref, k, mask in blocks:
        source = me ^ mask
        flags = ref[k, leaves * rank : leaves * rank + 8, :].astype(jnp.float32)
        projected = [ref[k, y * rank : (y + 1) * rank, :] for y in range(leaves)]
        chosen = []
        for c in range(slots):
            flag = jnp.sum(
                jnp.where(lane8 == me * slots + c, flags, 0.0), axis=1, keepdims=True
            )[0:1, :]
            flag = jnp.broadcast_to(flag, (1, 256))
            chosen.append(
                sum(
                    projected[y] * jnp.where(flag == y, 1.0, 0.0).astype(jnp.bfloat16)
                    for y in range(leaves)
                )
            )
        matrix = couplings_ref[source]
        routed = []
        for l in range(leaves):
            weight = jnp.zeros((1, slots * rank), jnp.float32)
            for c in range(slots):
                hit = jnp.where(dest_ref[source, c] == l, 1.0, 0.0)
                weight = jnp.where((lane >= c * rank) & (lane < (c + 1) * rank), hit, weight)
            routed.append(matrix * weight.astype(jnp.bfloat16))
        total = total + dot(jnp.concatenate(routed, 0), jnp.concatenate(chosen, 0))
    coeff = total.astype(jnp.bfloat16)
    for l in range(leaves):
        far = dot_t(basis_ref[l], coeff[l * rank : (l + 1) * rank, :])
        at = slice(l * rows, (l + 1) * rows)
        samples_ref[at, :] = (near_ref[at, :] + far).astype(jnp.bfloat16)
    left, right = samples_ref[:, 0:128], samples_ref[:, 128:256]
    top = dot_t(left, samples_ref[...])
    gram_ref[...] = pack(top, dot_t(right, right))


def rb(x,k): return jnp.broadcast_to(x[k:k+1,:],(8,128))

def split(a):
    h=a.astype(jnp.bfloat16); return h,(a-h.astype(jnp.float32)).astype(jnp.bfloat16)
def dg(a,b,dims): return lax.dot_general(a,b,(dims,((),())),preferred_element_type=jnp.float32)
def mm3(a,b,dims):
    ah,al=split(a); bh,bl=split(b)
    return dg(ah,bh,dims)+dg(ah,bl,dims)+dg(al,bh,dims)
def mm(a,b): return mm3(a,b,((1,),(0,)))
def mmt(a,b): return mm3(a,b,((1,),(1,)))
def eliminate(P, lane, row):
    base=lane & ~31
    sub=lane & 31
    V=[jnp.where(row+8*rv==sub,1.0,0.0).astype(jnp.float32) for rv in range(4)]
    P=list(P)
    for m in range(4):
        C=[[jnp.take_along_axis(P[rv],base+(8*m+k),axis=1,mode="promise_in_bounds") for rv in range(m,4)] for k in range(8)]
        piv=jnp.ones((8,128),jnp.float32)
        for k in range(8):
            d=rb(C[k][0],k)
            piv=jnp.where(row==k,d,piv)
            inv=1.0/d
            M=[c*inv for c in C[k]]
            M[0]=jnp.where(row>k,M[0],0.0)
            for k2 in range(k+1,8):
                f=rb(C[k2][0],k)
                C[k2]=[c-mu*f for c,mu in zip(C[k2],M)]
            fp=rb(P[m],k); fv=rb(V[m],k)
            for rv in range(m,4):
                P[rv]=P[rv]-M[rv-m]*fp
                V[rv]=V[rv]-M[rv-m]*fv
        rs=lax.rsqrt(piv)
        P[m]=P[m]*rs
        V[m]=V[m]*rs
    return P,V

def factor_kernel(seg_ref, mine_ref, other_ref, r_ref, tr_ref, X, Rb, Wb):
    lane=lax.broadcasted_iota(jnp.int32,(8,128),1); row=lax.broadcasted_iota(jnp.int32,(8,128),0)
    grp=lane//32
    l32=lax.broadcasted_iota(jnp.int32,(32,256),1)
    r32=lax.broadcasted_iota(jnp.int32,(32,256),0)
    bd=(lax.broadcasted_iota(jnp.int32,(128,128),0)//32)==(lax.broadcasted_iota(jnp.int32,(128,128),1)//32)
    l256=lax.broadcasted_iota(jnp.int32,(128,256),1); r256=lax.broadcasted_iota(jnp.int32,(128,256),0)&31
    odd = (lax.axis_index("sub") % 2) == 1
    mine, other = mine_ref[...], other_ref[...]
    first = jnp.where(odd, other, mine)
    second = jnp.where(odd, mine[0], other[0])
    levels = [seg_ref[...], first[0], first[1], (first[1] + second) * 0.5]
    for t, packed in enumerate(levels):
        rows = unpack(packed)
        for kb in range(8):
            X[kb, 32 * t : 32 * t + 32, :] = rows[32 * kb : 32 * kb + 32, :]
    for kb in range(8):
        off=32*kb; c0=off//128*128; lo=off%128
        P=[]
        for rv in range(4):
            acc=None
            for t in range(4):
                v=X[kb,t*32+8*rv:t*32+8*rv+8,c0:c0+128]
                sh=(32*t-lo)%128
                if sh: v=pltpu.roll(v,sh,1)
                acc=v if acc is None else jnp.where(grp==t,v,acc)
            P.append(acc)
        P,V=eliminate(P,lane,row)
        Pf=jnp.concatenate(P,0); Vf=jnp.concatenate(V,0)
        Wbd=jnp.where(bd,jnp.concatenate([Vf]*4,0),0.0)
        x=X[kb]
        x=jnp.where((l256>=off)&(l256<off+32),jnp.where(l256-off==r256,1.0,0.0),x)
        panel=mm(Wbd,x)
        chunks={}
        for i in range(kb+1,8):
            c=i//4
            if c not in chunks: chunks[c]=jnp.transpose(panel[:,c*128:c*128+128])
            T=chunks[c][(i%4)*32:(i%4)*32+32,:]
            L=jnp.where(bd,jnp.concatenate([T]*4,0),0.0)
            X[i]=jnp.where((l256>=off)&(l256<off+32),0.0,X[i])-mm(L,panel)
        for t in range(4):
            pt=panel[32*t:32*t+32,:]
            sh=(lo-32*t)%128
            d=Pf
            if sh: d=pltpu.roll(d,sh,1)
            d2=jnp.concatenate([d,d],1)
            Rb[t,off:off+32,:]=jnp.where(l32>=off+32,pt,jnp.where((l32>=off)&(l32-off>=r32),d2,0.0))
            if t>0: Wb[t-1,off:off+32,:]=jnp.where(l32<off+32,pt,0.0)
    r_ref[...]=Rb[0]
    for t in range(3):
        tr_ref[t]=mmt(Rb[t],Wb[t]).astype(jnp.bfloat16)

def factor_all(seg_gram, mine, other):
    return pl.pallas_call(
        factor_kernel,
        out_shape=(
            jax.ShapeDtypeStruct((256, 256), jnp.float32),
            jax.ShapeDtypeStruct((LEVELS, 256, 256), jnp.bfloat16),
        ),
        in_specs=[VMEM] * 3,
        out_specs=[VMEM] * 2,
        scratch_shapes=[
            pltpu.VMEM((8, 128, 256), jnp.float32),
            pltpu.VMEM((4, 256, 256), jnp.float32),
            pltpu.VMEM((3, 256, 256), jnp.float32),
        ],
        compiler_params=params(),
    )(seg_gram, mine, other)


def body(
    near_blocks, sample_cols, near_list, row_basis_t, col_basis_t, couplings, far_source, far_dest
):
    leaf_count, near_count, leaf_rows, _ = near_blocks.shape
    width = sample_cols.shape[1]
    rank = row_basis_t.shape[1]
    n_seg, n_sub = lax.axis_size("seg"), lax.axis_size("sub")
    n = n_seg * n_sub
    rows = leaf_count * leaf_rows

    swap = lax.ppermute(sample_cols, AXES, [(i, i ^ 1) for i in range(n)])
    ahead = [(i, i + 1) for i in range(1, n - 1, 2)]
    cross = lax.ppermute(sample_cols, AXES, ahead + [(j, i) for i, j in ahead])

    mine = pl.pallas_call(
        project_kernel,
        out_shape=jax.ShapeDtypeStruct((1, leaf_count * rank + 8, width), jnp.bfloat16),
        in_specs=[VMEM, VMEM, SMEM],
        out_specs=VMEM,
        compiler_params=params(),
        cost_estimate=pl.CostEstimate(
            flops=2 * rows * rank * width, bytes_accessed=512 * 2**10, transcendentals=0
        ),
    )(col_basis_t, sample_cols, far_source[0, 0])

    high = [hop(mine, m, m) for m in range(4, n_seg, 4)]
    low = [hop(mine, m, m) for m in (1, 2, 3)]
    column = jnp.concatenate(high, 0)
    rest = [hop(column, m, m) for m in (1, 2, 3)]

    near_part = pl.pallas_call(
        near_kernel,
        grid=(leaf_count,),
        out_shape=jax.ShapeDtypeStruct((rows, width), jnp.float32),
        in_specs=[
            SMEM,
            pl.BlockSpec((1, near_count, leaf_rows, leaf_rows), lambda i: (i, 0, 0, 0)),
            VMEM,
            VMEM,
            VMEM,
        ],
        out_specs=pl.BlockSpec((leaf_rows, width), lambda i: (i, 0)),
        scratch_shapes=[pltpu.VMEM((3 * leaf_count + 1, leaf_rows, width), jnp.bfloat16)],
        compiler_params=params(),
        cost_estimate=pl.CostEstimate(
            flops=2 * rows * near_count * leaf_rows * width,
            bytes_accessed=near_blocks.size * 2 + 5 * rows * width * 2,
            transcendentals=0,
        ),
    )(near_list, near_blocks, sample_cols, swap, cross)

    samples, gram = pl.pallas_call(
        combine_kernel,
        out_shape=(
            jax.ShapeDtypeStruct((rows, width), jnp.bfloat16),
            jax.ShapeDtypeStruct((320, 128), jnp.float32),
        ),
        in_specs=[SMEM] + [VMEM] * 11,
        out_specs=[VMEM] * 2,
        compiler_params=params(),
    )(far_dest[0, 0], couplings[0, 0], row_basis_t, near_part, mine, *low, column, *rest)

    total, mask = gram, 1
    while mask < n_sub:
        total = total + sub_hop(total, mask)
        mask *= 2
    seg_gram = total / (n_sub * rows)
    rounded = seg_gram.astype(jnp.bfloat16)
    got = [
        hop(rounded, *masks).astype(jnp.float32) for masks in ((1, 4), (2, 6), (3, 5), (None, 7))
    ]
    odd = (lax.axis_index("sub") % 2) == 1
    pair = seg_gram + got[0]
    quad = (got[1] + got[2]) + pair
    far_quad = (got[0] + got[1]) + (got[2] + got[3])
    sent = jnp.stack([jnp.where(odd, far_quad * 0.25, pair * 0.5), quad * 0.25])
    received = sub_hop(sent, 1)
    segment_factor, transfers = factor_all(seg_gram, sent, received)
    return (samples, segment_factor, transfers[None])


def solution(mesh):
    in_specs = (
        P(("seg", "sub"), None, None, None),
        P(("seg", "sub"), None),
        P(("seg", "sub"), None),
        P(("seg", "sub"), None, None),
        P(("seg", "sub"), None, None),
        P("seg", "sub", None, None, None),
        P("seg", "sub", None, None),
        P("seg", "sub", None, None),
    )
    out_specs = (P(("seg", "sub"), None), P("seg", None), P("seg", None, None, None))
    return jax.shard_map(body, mesh=mesh, in_specs=in_specs, out_specs=out_specs, check_vma=False)
```

```python
import functools

import jax
import jax.numpy as jnp
from jax import lax
from jax.experimental import pallas as pl
from jax.experimental.pallas import tpu as pltpu
from jax.sharding import PartitionSpec as P

LEVELS = 3
PLANE = 4
FIRST_KIB = 61440
AXES = ("seg", "sub")
VMEM = pl.BlockSpec(memory_space=pltpu.VMEM)
SMEM = pl.BlockSpec(memory_space=pltpu.SMEM)


def params(kib=48 * 2**10):
    return pltpu.CompilerParams(vmem_limit_bytes=kib * 2**10)


def hop(value, even, odd):
    n_seg, n_sub = lax.axis_size("seg"), lax.axis_size("sub")
    pairs = []
    for s in range(n_seg):
        for u in range(n_sub):
            mask = odd if u % 2 else even
            if mask:
                pairs.append((s * n_sub + u, (s ^ mask) * n_sub + u))
    return lax.ppermute(value, AXES, pairs)


def sub_hop(value, mask):
    return lax.ppermute(value, "sub", [(i, i ^ mask) for i in range(lax.axis_size("sub"))])


def pack(top, low):
    lane = lax.broadcasted_iota(jnp.int32, (64, 128), 1)
    corner = pltpu.roll(low[64:128, :], 64, 1)
    mixed = jnp.where(lane < 64, corner, top[64:128, 0:128])
    return jnp.concatenate([top[0:64, 0:128], mixed, top[:, 128:256], low[0:64, :]], 0)


def unpack(packed):
    zero = jnp.zeros((64, 128), jnp.float32)
    left = jnp.concatenate([packed[0:128, :], zero, zero], 0)
    right = jnp.concatenate(
        [packed[128:256, :], packed[256:320, :], pltpu.roll(packed[64:128, :], 64, 1)], 0
    )
    return jnp.concatenate([left, right], 1)


def dot(a, b):
    return jnp.dot(a, b, preferred_element_type=jnp.float32)


def dot_t(a, b):
    return lax.dot_general(a, b, (((0,), (0,)), ((), ())), preferred_element_type=jnp.float32)


def first_kernel(basis_hbm, cols_hbm, couplings_hbm, row_hbm, source_ref, dest_ref, *rest):
    mine_ref, row_ref, *pay_refs, basis, cols, couplings, flags, sems = rest
    copies = [
        pltpu.make_async_copy(src, dst, sems.at[i])
        for i, (src, dst) in enumerate(
            ((basis_hbm, basis), (cols_hbm, cols), (couplings_hbm.at[0, 0], couplings), (row_hbm, row_ref))
        )
    ]
    for copy in copies:
        copy.start()
    slots, peers = source_ref.shape
    leaves, rank, rows = basis.shape
    for i, ref in enumerate((source_ref, dest_ref)):
        flags[i] = jnp.zeros(flags.shape[1:], jnp.float32)
        flags[i, 0:slots, 0:peers] = ref[...].astype(jnp.float32)
    copies[0].wait()
    copies[1].wait()
    for l in range(leaves):
        mine_ref[0, l * rank : (l + 1) * rank, :] = dot(
            basis[l], cols[l * rows : (l + 1) * rows, :]
        ).astype(jnp.bfloat16)
    mine_ref[0, leaves * rank : leaves * rank + 8, :] = flags[0].astype(jnp.bfloat16)
    copies[2].wait()
    copies[3].wait()
    me = lax.axis_index("seg")
    high = peers // PLANE
    for m, pay in enumerate(pay_refs):
        for z in range(high):
            pay[0, z * rank : (z + 1) * rank, :] = couplings[z * PLANE + (me ^ m) % PLANE]
        pay[0, high * rank : high * rank + 8, :] = flags[1, :, 0:128].astype(jnp.bfloat16)


def partial_kernel(leaves, slots, *refs):
    high = len(refs) - 2 * PLANE
    blocks, couplings, outs = refs[:high], refs[high : high + PLANE], refs[high + PLANE :]
    rank = (blocks[0].shape[1] - 8) // leaves
    me = lax.axis_index("seg")
    lane8 = lax.broadcasted_iota(jnp.int32, (8, 128), 1)
    lane = lax.broadcasted_iota(jnp.int32, (1, slots * rank), 1)

    def pick(flags, index):
        return jnp.sum(jnp.where(lane8 == index, flags, 0.0), axis=1, keepdims=True)

    sources = [ref[0, leaves * rank : leaves * rank + 8, 0:128].astype(jnp.float32) for ref in blocks]
    for m in range(PLANE):
        target = me ^ m
        dests = couplings[m][0, high * rank : high * rank + 8, :].astype(jnp.float32)
        total = jnp.zeros((leaves * rank, 256), jnp.float32)
        for k in range(high):
            source = pick(sources[k], target)
            dest = pick(dests, me ^ (PLANE * k))
            chosen = []
            for c in range(slots):
                flag = jnp.broadcast_to(source[c : c + 1, :], (1, 256))
                chosen.append(
                    sum(
                        blocks[k][0, y * rank : (y + 1) * rank, :]
                        * jnp.where(flag == y, 1.0, 0.0).astype(jnp.bfloat16)
                        for y in range(leaves)
                    )
                )
            at = pl.multiple_of(((me // PLANE) ^ k) * rank, rank)
            matrix = couplings[m][0, pl.ds(at, rank), :]
            wide = jnp.broadcast_to(dest[0:1, :], lane.shape)
            for c in range(1, slots):
                wide = jnp.where(lane >= c * rank, dest[c : c + 1, :], wide)
            routed = [
                matrix * jnp.where(wide == l, 1.0, 0.0).astype(jnp.bfloat16) for l in range(leaves)
            ]
            total = total + dot(jnp.concatenate(routed, 0), jnp.concatenate(chosen, 0))
        outs[m][0] = total.astype(outs[m].dtype)


def near_kernel(list_ref, blocks_ref, own_ref, swap_ref, cross_ref, out_ref, held):
    leaf = pl.program_id(0)
    leaves = held.shape[0] // 3

    @pl.when(leaf == 0)
    def _():
        for j in range(leaves):
            rows = slice(j * 256, (j + 1) * 256)
            held[j] = own_ref[rows, :]
            held[leaves + j] = swap_ref[rows, :]
            held[2 * leaves + j] = cross_ref[rows, :]
        held[3 * leaves] = jnp.zeros_like(held[0])

    device = lax.axis_index("seg") * lax.axis_size("sub") + lax.axis_index("sub")
    odd = device % 2
    before = (2 - odd) * leaves
    after = (1 + odd) * leaves
    acc = jnp.zeros((256, 256), jnp.float32)
    for k in range(blocks_ref.shape[1]):
        entry = list_ref[leaf, k]
        shift = entry - device * leaves
        slot = jnp.where(
            shift < 0, before + leaves + shift, jnp.where(shift < leaves, shift, after + shift - leaves)
        )
        slot = jnp.where(entry < 0, 3 * leaves, slot)
        acc = acc + dot(blocks_ref[0, k], held[slot])
    out_ref[...] = acc


def combine_kernel(basis_ref, near_ref, own_ref, *refs):
    *got, samples_ref, gram_ref = refs
    leaves, rank, rows = basis_ref.shape
    total = own_ref[0]
    for ref in got:
        total = total + ref[0].astype(jnp.float32)
    coeff = total.astype(jnp.bfloat16)
    for l in range(leaves):
        far = dot_t(basis_ref[l], coeff[l * rank : (l + 1) * rank, :])
        at = slice(l * rows, (l + 1) * rows)
        samples_ref[at, :] = (near_ref[at, :] + far).astype(jnp.bfloat16)
    left, right = samples_ref[:, 0:128], samples_ref[:, 128:256]
    top = dot_t(left, samples_ref[...])
    gram_ref[...] = pack(top, dot_t(right, right))


def rb(x,k): return jnp.broadcast_to(x[k:k+1,:],(8,128))

def split(a):
    h=a.astype(jnp.bfloat16); return h,(a-h.astype(jnp.float32)).astype(jnp.bfloat16)
def dg(a,b,dims): return lax.dot_general(a,b,(dims,((),())),preferred_element_type=jnp.float32)
def lstack(a):
    h,l=split(a); return jnp.concatenate([h,l,h],1)
def rstack(b):
    h,l=split(b); return jnp.concatenate([h,h,l],0)
def mms(a,b): return dg(a,b,((1,),(0,)))
def mmt(a,b):
    ah,al=split(a); bh,bl=split(b)
    return dg(jnp.concatenate([ah,al,ah],1),jnp.concatenate([bh,bh,bl],1),((1,),(1,)))
def eliminate(P, lane, row):
    base=lane & ~31
    sub=lane & 31
    V=[jnp.where(row+8*rv==sub,1.0,0.0).astype(jnp.float32) for rv in range(4)]
    P=list(P)
    for m in range(4):
        C=[[jnp.take_along_axis(P[rv],base+(8*m+k),axis=1,mode="promise_in_bounds") for rv in range(m,4)] for k in range(8)]
        piv=jnp.ones((8,128),jnp.float32)
        for k in range(8):
            d=rb(C[k][0],k)
            piv=jnp.where(row==k,d,piv)
            inv=1.0/d
            M=[c*inv for c in C[k]]
            M[0]=jnp.where(row>k,M[0],0.0)
            for k2 in range(k+1,8):
                f=rb(C[k2][0],k)
                C[k2]=[c-mu*f for c,mu in zip(C[k2],M)]
            fp=rb(P[m],k); fv=rb(V[m],k)
            for rv in range(m,4):
                P[rv]=P[rv]-M[rv-m]*fp
                V[rv]=V[rv]-M[rv-m]*fv
        rs=lax.rsqrt(piv)
        P[m]=P[m]*rs
        V[m]=V[m]*rs
    return P,V

def factor_kernel(seg_ref, mine_ref, other_ref, r_ref, tr_ref, X, Rb, Wb):
    lane=lax.broadcasted_iota(jnp.int32,(8,128),1); row=lax.broadcasted_iota(jnp.int32,(8,128),0)
    grp=lane//32
    l32=lax.broadcasted_iota(jnp.int32,(32,256),1)
    r32=lax.broadcasted_iota(jnp.int32,(32,256),0)
    bd=(lax.broadcasted_iota(jnp.int32,(128,128),0)//32)==(lax.broadcasted_iota(jnp.int32,(128,128),1)//32)
    l256=lax.broadcasted_iota(jnp.int32,(128,256),1); r256=lax.broadcasted_iota(jnp.int32,(128,256),0)&31
    odd = (lax.axis_index("sub") % 2) == 1
    mine, other = mine_ref[...], other_ref[...]
    first = jnp.where(odd, other, mine)
    second = jnp.where(odd, mine[0], other[0])
    levels = [seg_ref[...], first[0], first[1], (first[1] + second) * 0.5]
    for t, packed in enumerate(levels):
        rows = unpack(packed)
        for kb in range(8):
            X[kb, 32 * t : 32 * t + 32, :] = rows[32 * kb : 32 * kb + 32, :]
    for kb in range(8):
        off=32*kb; c0=off//128*128; lo=off%128
        P=[]
        for rv in range(4):
            acc=None
            for t in range(4):
                v=X[kb,t*32+8*rv:t*32+8*rv+8,c0:c0+128]
                sh=(32*t-lo)%128
                if sh: v=pltpu.roll(v,sh,1)
                acc=v if acc is None else jnp.where(grp==t,v,acc)
            P.append(acc)
        P,V=eliminate(P,lane,row)
        Pf=jnp.concatenate(P,0); Vf=jnp.concatenate(V,0)
        Wbd=jnp.where(bd,jnp.concatenate([Vf]*4,0),0.0)
        x=X[kb]
        x=jnp.where((l256>=off)&(l256<off+32),jnp.where(l256-off==r256,1.0,0.0),x)
        panel=mms(lstack(Wbd),rstack(x)); ps=rstack(panel)
        chunks={}
        for i in range(kb+1,8):
            c=i//4
            if c not in chunks: chunks[c]=jnp.transpose(panel[:,c*128:c*128+128])
            T=chunks[c][(i%4)*32:(i%4)*32+32,:]
            L=jnp.where(bd,jnp.concatenate([T]*4,0),0.0)
            X[i]=jnp.where((l256>=off)&(l256<off+32),0.0,X[i])-mms(lstack(L),ps)
        for t in range(4):
            pt=panel[32*t:32*t+32,:]
            sh=(lo-32*t)%128
            d=Pf
            if sh: d=pltpu.roll(d,sh,1)
            d2=jnp.concatenate([d,d],1)
            Rb[t,off:off+32,:]=jnp.where(l32>=off+32,pt,jnp.where((l32>=off)&(l32-off>=r32),d2,0.0))
            if t>0: Wb[t-1,off:off+32,:]=jnp.where(l32<off+32,pt,0.0)
    r_ref[...]=Rb[0]
    for t in range(3):
        tr_ref[t]=mmt(Rb[t],Wb[t]).astype(jnp.bfloat16)

def factor_all(seg_gram, mine, other):
    return pl.pallas_call(
        factor_kernel,
        out_shape=(
            jax.ShapeDtypeStruct((256, 256), jnp.float32),
            jax.ShapeDtypeStruct((LEVELS, 256, 256), jnp.bfloat16),
        ),
        in_specs=[VMEM] * 3,
        out_specs=[VMEM] * 2,
        scratch_shapes=[
            pltpu.VMEM((8, 128, 256), jnp.float32),
            pltpu.VMEM((4, 256, 256), jnp.float32),
            pltpu.VMEM((3, 256, 256), jnp.float32),
        ],
        compiler_params=params(),
    )(seg_gram, mine, other)


def body(
    near_blocks, sample_cols, near_list, row_basis_t, col_basis_t, couplings, far_source, far_dest
):
    leaf_count, near_count, leaf_rows, _ = near_blocks.shape
    width = sample_cols.shape[1]
    rank = row_basis_t.shape[1]
    n_seg, n_sub = lax.axis_size("seg"), lax.axis_size("sub")
    n = n_seg * n_sub
    rows = leaf_count * leaf_rows

    swap = lax.ppermute(sample_cols, AXES, [(i, i ^ 1) for i in range(n)])
    ahead = [(i, i + 1) for i in range(1, n - 1, 2)]
    cross = lax.ppermute(sample_cols, AXES, ahead + [(j, i) for i, j in ahead])

    slots = far_source.shape[3]
    basis_first, swap = lax.optimization_barrier((col_basis_t, swap))
    high = n_seg // PLANE
    hbm = pl.BlockSpec(memory_space=pltpu.HBM)
    bf16 = jnp.bfloat16
    mine, row_basis, *pays = pl.pallas_call(
        first_kernel,
        out_shape=[
            jax.ShapeDtypeStruct((1, leaf_count * rank + 8, width), bf16),
            jax.ShapeDtypeStruct(row_basis_t.shape, bf16),
        ]
        + [jax.ShapeDtypeStruct((1, high * rank + 8, slots * rank), bf16)] * PLANE,
        in_specs=[hbm] * 4 + [VMEM] * 2,
        out_specs=[VMEM] * (2 + PLANE),
        scratch_shapes=[
            pltpu.VMEM(col_basis_t.shape, bf16),
            pltpu.VMEM(sample_cols.shape, bf16),
            pltpu.VMEM(couplings.shape[2:], bf16),
            pltpu.VMEM((2, 8, 256), jnp.float32),
            pltpu.SemaphoreType.DMA((4,)),
        ],
        compiler_params=params(FIRST_KIB),
    )(
        basis_first,
        sample_cols,
        couplings,
        row_basis_t,
        jnp.swapaxes(far_source[0, 0], 0, 1),
        jnp.swapaxes(far_dest[0, 0], 0, 1),
    )

    column = [hop(mine, PLANE * k, PLANE * k) for k in range(1, high)]
    gathered = [hop(pays[m], m, m) for m in range(1, PLANE)]
    near_part = pl.pallas_call(
        near_kernel,
        grid=(leaf_count,),
        out_shape=jax.ShapeDtypeStruct((rows, width), jnp.float32),
        in_specs=[
            SMEM,
            pl.BlockSpec((1, near_count, leaf_rows, leaf_rows), lambda i: (i, 0, 0, 0)),
            VMEM,
            VMEM,
            VMEM,
        ],
        out_specs=pl.BlockSpec((leaf_rows, width), lambda i: (i, 0)),
        scratch_shapes=[pltpu.VMEM((3 * leaf_count + 1, leaf_rows, width), jnp.bfloat16)],
        compiler_params=params(),
        cost_estimate=pl.CostEstimate(
            flops=2 * rows * near_count * leaf_rows * width,
            bytes_accessed=near_blocks.size * 2 + 5 * rows * width * 2,
            transcendentals=0,
        ),
    )(near_list, near_blocks, sample_cols, swap, cross)
    column, gathered, near_part = lax.optimization_barrier((column, gathered, near_part))
    own, *parts = pl.pallas_call(
        functools.partial(partial_kernel, leaf_count, slots),
        out_shape=[jax.ShapeDtypeStruct((1, leaf_count * rank, width), jnp.float32)]
        + [jax.ShapeDtypeStruct((1, leaf_count * rank, width), bf16)] * (PLANE - 1),
        in_specs=[VMEM] * (PLANE + high),
        out_specs=[VMEM] * PLANE,
        compiler_params=params(),
    )(mine, *column, pays[0], *gathered)
    got = [hop(parts[m - 1], m, m) for m in range(1, PLANE)]

    samples, gram = pl.pallas_call(
        combine_kernel,
        out_shape=(
            jax.ShapeDtypeStruct((rows, width), jnp.bfloat16),
            jax.ShapeDtypeStruct((320, 128), jnp.float32),
        ),
        in_specs=[VMEM] * (3 + PLANE - 1),
        out_specs=[VMEM] * 2,
        compiler_params=params(),
    )(row_basis, near_part, own, *got)

    total, mask = gram, 1
    while mask < n_sub:
        total = total + sub_hop(total, mask)
        mask *= 2
    seg_gram = total / (n_sub * rows)
    rounded = seg_gram.astype(jnp.bfloat16)
    near = [
        hop(rounded, *masks).astype(jnp.float32) for masks in ((1, 4), (2, 6), (3, 5), (None, 7))
    ]
    odd = (lax.axis_index("sub") % 2) == 1
    pair = seg_gram + near[0]
    quad = (near[1] + near[2]) + pair
    far_quad = (near[0] + near[1]) + (near[2] + near[3])
    sent = jnp.stack([jnp.where(odd, far_quad * 0.25, pair * 0.5), quad * 0.25])
    received = sub_hop(sent, 1)
    segment_factor, transfers = factor_all(seg_gram, sent, received)
    return (samples, segment_factor, transfers[None])


def solution(mesh):
    in_specs = (
        P(("seg", "sub"), None, None, None),
        P(("seg", "sub"), None),
        P(("seg", "sub"), None),
        P(("seg", "sub"), None, None),
        P(("seg", "sub"), None, None),
        P("seg", "sub", None, None, None),
        P("seg", "sub", None, None),
        P("seg", "sub", None, None),
    )
    out_specs = (P(("seg", "sub"), None), P("seg", None), P("seg", None, None, None))
    return jax.shard_map(body, mesh=mesh, in_specs=in_specs, out_specs=out_specs, check_vma=False)
```

```python
import functools

import jax
import jax.numpy as jnp
from jax import lax
from jax.experimental import pallas as pl
from jax.experimental.pallas import tpu as pltpu
from jax.sharding import PartitionSpec as P

LEVELS = 3
PLANE = 4
NEAR_KIB = 49152
FIRST_KIB = 61440
AXES = ("seg", "sub")
VMEM = pl.BlockSpec(memory_space=pltpu.VMEM)
SMEM = pl.BlockSpec(memory_space=pltpu.SMEM)


def params(kib=48 * 2**10):
    return pltpu.CompilerParams(vmem_limit_bytes=kib * 2**10)


def hop(value, even, odd):
    n_seg, n_sub = lax.axis_size("seg"), lax.axis_size("sub")
    pairs = []
    for s in range(n_seg):
        for u in range(n_sub):
            mask = odd if u % 2 else even
            if mask:
                pairs.append((s * n_sub + u, (s ^ mask) * n_sub + u))
    return lax.ppermute(value, AXES, pairs)


def sub_hop(value, mask):
    return lax.ppermute(value, "sub", [(i, i ^ mask) for i in range(lax.axis_size("sub"))])


def pack(top, low):
    lane = lax.broadcasted_iota(jnp.int32, (64, 128), 1)
    corner = pltpu.roll(low[64:128, :], 64, 1)
    mixed = jnp.where(lane < 64, corner, top[64:128, 0:128])
    return jnp.concatenate([top[0:64, 0:128], mixed, top[:, 128:256], low[0:64, :]], 0)


def unpack(packed):
    zero = jnp.zeros((64, 128), jnp.float32)
    left = jnp.concatenate([packed[0:128, :], zero, zero], 0)
    right = jnp.concatenate(
        [packed[128:256, :], packed[256:320, :], pltpu.roll(packed[64:128, :], 64, 1)], 0
    )
    return jnp.concatenate([left, right], 1)


def dot(a, b):
    return jnp.dot(a, b, preferred_element_type=jnp.float32)


def dot_t(a, b):
    return lax.dot_general(a, b, (((0,), (0,)), ((), ())), preferred_element_type=jnp.float32)


def first_kernel(basis_hbm, cols_hbm, couplings_hbm, row_hbm, source_ref, dest_ref, *rest):
    mine_ref, row_ref, *pay_refs, basis, cols, couplings, flags, sems = rest
    copies = [
        pltpu.make_async_copy(src, dst, sems.at[i])
        for i, (src, dst) in enumerate(
            ((basis_hbm, basis), (cols_hbm, cols), (couplings_hbm.at[0, 0], couplings), (row_hbm, row_ref))
        )
    ]
    for copy in copies:
        copy.start()
    slots, peers = source_ref.shape
    leaves, rank, rows = basis.shape
    for i, ref in enumerate((source_ref, dest_ref)):
        flags[i] = jnp.zeros(flags.shape[1:], jnp.float32)
        flags[i, 0:slots, 0:peers] = ref[...].astype(jnp.float32)
    copies[0].wait()
    copies[1].wait()
    for l in range(leaves):
        mine_ref[0, l * rank : (l + 1) * rank, :] = dot(
            basis[l], cols[l * rows : (l + 1) * rows, :]
        ).astype(jnp.bfloat16)
    mine_ref[0, leaves * rank : leaves * rank + 8, :] = flags[0].astype(jnp.bfloat16)
    copies[2].wait()
    copies[3].wait()
    me = lax.axis_index("seg")
    high = peers // PLANE
    for m, pay in enumerate(pay_refs):
        for z in range(high):
            pay[0, z * rank : (z + 1) * rank, :] = couplings[z * PLANE + (me ^ m) % PLANE]
        pay[0, high * rank : high * rank + 8, :] = flags[1, :, 0:128].astype(jnp.bfloat16)


def partial_kernel(leaves, slots, *refs):
    high = len(refs) - 2 * PLANE
    blocks, couplings, outs = refs[:high], refs[high : high + PLANE], refs[high + PLANE :]
    rank = (blocks[0].shape[1] - 8) // leaves
    me = lax.axis_index("seg")
    lane8 = lax.broadcasted_iota(jnp.int32, (8, 128), 1)
    lane = lax.broadcasted_iota(jnp.int32, (1, slots * rank), 1)

    def pick(flags, index):
        return jnp.sum(jnp.where(lane8 == index, flags, 0.0), axis=1, keepdims=True)

    sources = [ref[0, leaves * rank : leaves * rank + 8, 0:128].astype(jnp.float32) for ref in blocks]
    for m in range(PLANE):
        target = me ^ m
        dests = couplings[m][0, high * rank : high * rank + 8, :].astype(jnp.float32)
        total = jnp.zeros((leaves * rank, 256), jnp.float32)
        for k in range(high):
            source = pick(sources[k], target)
            dest = pick(dests, me ^ (PLANE * k))
            chosen = []
            for c in range(slots):
                flag = jnp.broadcast_to(source[c : c + 1, :], (1, 256))
                chosen.append(
                    sum(
                        blocks[k][0, y * rank : (y + 1) * rank, :]
                        * jnp.where(flag == y, 1.0, 0.0).astype(jnp.bfloat16)
                        for y in range(leaves)
                    )
                )
            at = pl.multiple_of(((me // PLANE) ^ k) * rank, rank)
            matrix = couplings[m][0, pl.ds(at, rank), :]
            wide = jnp.broadcast_to(dest[0:1, :], lane.shape)
            for c in range(1, slots):
                wide = jnp.where(lane >= c * rank, dest[c : c + 1, :], wide)
            routed = [
                matrix * jnp.where(wide == l, 1.0, 0.0).astype(jnp.bfloat16) for l in range(leaves)
            ]
            total = total + dot(jnp.concatenate(routed, 0), jnp.concatenate(chosen, 0))
        outs[m][0] = total.astype(outs[m].dtype)


def near_kernel(list_hbm, blocks_ref, own_hbm, swap_ref, cross_ref, out_ref, held, entries, sems):
    leaves, count, rows, _ = blocks_ref.shape
    pairs = [(list_hbm, entries)]
    pairs += [(own_hbm.at[pl.ds(j * rows, rows)], held.at[j]) for j in range(leaves)]
    copies = [pltpu.make_async_copy(src, dst, sems.at[i]) for i, (src, dst) in enumerate(pairs)]
    for copy in copies:
        copy.start()
    for i, src in enumerate((swap_ref, cross_ref)):
        for j in range(leaves):
            held[(i + 1) * leaves + j] = src[j * rows : (j + 1) * rows, :]
    held[3 * leaves] = jnp.zeros(held.shape[1:], held.dtype)
    for copy in copies:
        copy.wait()
    device = lax.axis_index("seg") * lax.axis_size("sub") + lax.axis_index("sub")
    odd = device % 2
    before = (2 - odd) * leaves
    after = (1 + odd) * leaves
    for l in range(leaves):
        acc = jnp.zeros((rows, held.shape[2]), jnp.float32)
        for k in range(count):
            entry = entries[l, k]
            shift = entry - device * leaves
            outside = jnp.where(shift < 0, before + leaves + shift, after + shift - leaves)
            slot = jnp.where((shift < 0) | (shift >= leaves), outside, shift)
            slot = jnp.where(entry < 0, 3 * leaves, slot)
            acc = acc + dot(blocks_ref[l, k], held[slot])
        out_ref[l * rows : (l + 1) * rows, :] = acc


def combine_kernel(basis_ref, near_ref, own_ref, *refs):
    *got, samples_ref, gram_ref = refs
    leaves, rank, rows = basis_ref.shape
    total = own_ref[0]
    for ref in got:
        total = total + ref[0].astype(jnp.float32)
    coeff = total.astype(jnp.bfloat16)
    for l in range(leaves):
        far = dot_t(basis_ref[l], coeff[l * rank : (l + 1) * rank, :])
        at = slice(l * rows, (l + 1) * rows)
        samples_ref[at, :] = (near_ref[at, :] + far).astype(jnp.bfloat16)
    left, right = samples_ref[:, 0:128], samples_ref[:, 128:256]
    top = dot_t(left, samples_ref[...])
    gram_ref[...] = pack(top, dot_t(right, right))


def rb(x,k): return jnp.broadcast_to(x[k:k+1,:],(8,128))

def split(a):
    h=a.astype(jnp.bfloat16); return h,(a-h.astype(jnp.float32)).astype(jnp.bfloat16)
def dg(a,b,dims): return lax.dot_general(a,b,(dims,((),())),preferred_element_type=jnp.float32)
def lstack(a):
    h,l=split(a); return jnp.concatenate([h,l,h],1)
def rstack(b):
    h,l=split(b); return jnp.concatenate([h,h,l],0)
def mms(a,b): return dg(a,b,((1,),(0,)))
def mmt(a,b):
    ah,al=split(a); bh,bl=split(b)
    return dg(jnp.concatenate([ah,al,ah],1),jnp.concatenate([bh,bh,bl],1),((1,),(1,)))
def eliminate(P, lane, row, tick):
    base=lane & ~31
    sub=lane & 31
    V=[jnp.where(row+8*rv==sub,1.0,0.0).astype(jnp.float32) for rv in range(4)]
    P=list(P)
    for m in range(4):
        C=[[jnp.take_along_axis(P[rv],base+(8*m+k),axis=1,mode="promise_in_bounds") for rv in range(m,4)] for k in range(8)]
        piv=jnp.ones((8,128),jnp.float32)
        for k in range(8):
            d=rb(C[k][0],k)
            piv=jnp.where(row==k,d,piv)
            inv=1.0/d
            M=[c*inv for c in C[k]]
            M[0]=jnp.where(row>k,M[0],0.0)
            for k2 in range(k+1,8):
                f=rb(C[k2][0],k)
                C[k2]=[c-mu*f for c,mu in zip(C[k2],M)]
            fp=rb(P[m],k); fv=rb(V[m],k)
            for rv in range(m,4):
                P[rv]=P[rv]-M[rv-m]*fp
                V[rv]=V[rv]-M[rv-m]*fv
            tick(8*m+k)
        rs=lax.rsqrt(piv)
        P[m]=P[m]*rs
        V[m]=V[m]*rs
    return P,V

def factor_kernel(seg_ref, mine_ref, other_ref, r_ref, tr_ref, X, Rb, Wb):
    lane=lax.broadcasted_iota(jnp.int32,(8,128),1); row=lax.broadcasted_iota(jnp.int32,(8,128),0)
    grp=lane//32
    l32=lax.broadcasted_iota(jnp.int32,(32,256),1)
    r32=lax.broadcasted_iota(jnp.int32,(32,256),0)
    bd=(lax.broadcasted_iota(jnp.int32,(128,128),0)//32)==(lax.broadcasted_iota(jnp.int32,(128,128),1)//32)
    l256=lax.broadcasted_iota(jnp.int32,(128,256),1); r256=lax.broadcasted_iota(jnp.int32,(128,256),0)&31
    odd = (lax.axis_index("sub") % 2) == 1
    mine, other = mine_ref[...], other_ref[...]
    first = jnp.where(odd, other, mine)
    second = jnp.where(odd, mine[0], other[0])
    levels = [seg_ref[...], first[0], first[1], (first[1] + second) * 0.5]
    for t, packed in enumerate(levels):
        rows = unpack(packed)
        for kb in range(8):
            X[kb, 32 * t : 32 * t + 32, :] = rows[32 * kb : 32 * kb + 32, :]
    pending=[]
    def tick(step):
        if pending and step%2==2-1: pending.pop(0)()
    def update(i,L,ps,off):
        X[i]=jnp.where((l256>=off)&(l256<off+32),0.0,X[i])-mms(L,ps)
    def emit(kb,panel,Pf):
        off=32*kb; lo=off%128
        for t in range(4):
            pt=panel[32*t:32*t+32,:]
            sh=(lo-32*t)%128
            d=Pf
            if sh: d=pltpu.roll(d,sh,1)
            d2=jnp.concatenate([d,d],1)
            Rb[t,off:off+32,:]=jnp.where(l32>=off+32,pt,jnp.where((l32>=off)&(l32-off>=r32),d2,0.0))
            if t>0: Wb[t-1,off:off+32,:]=jnp.where(l32<off+32,pt,0.0)
    def place(rows_of, block, lo):
        out=[]
        for t in range(4):
            sh=(32*t-lo)%128
            v=rows_of(t)
            out.append(pltpu.roll(v,sh,1) if sh else v)
        return out
    def packed(block, kb_cols):
        off=32*kb_cols; c0=off//128*128; lo=off%128
        vs=place(lambda t:X[block,32*t:32*t+32,c0:c0+128],block,lo)
        acc=vs[0]
        for t in range(1,4): acc=jnp.where(grp32==t,vs[t],acc)
        return acc
    grp32=lax.broadcasted_iota(jnp.int32,(32,128),1)//32
    state={}
    def prep(kb):
        off=32*(kb+1); c0=off//128*128; lo=off%128
        q=jnp.concatenate(place(lambda t:X[kb,32*t:32*t+32,c0:c0+128],kb,lo),0)
        state['q']=rstack(jnp.where(bd,q,0.0))
        state['d']=packed(kb+1,kb+1)
    def make_panel(kb,Vf):
        off=32*kb
        Wbd=jnp.where(bd,jnp.concatenate([Vf]*4,0),0.0)
        x=X[kb]
        x=jnp.where((l256>=off)&(l256<off+32),jnp.where(l256-off==r256,1.0,0.0),x)
        state['panel']=mms(lstack(Wbd),rstack(x))
        state['ps']=rstack(state['panel'])
        state['ch']={}
    def go(i,off):
        c=i//4
        if c not in state['ch']: state['ch'][c]=jnp.transpose(state['panel'][:,c*128:c*128+128])
        T=state['ch'][c][(i%4)*32:(i%4)*32+32,:]
        update(i,lstack(jnp.where(bd,jnp.concatenate([T]*4,0),0.0)),state['ps'],off)
    def emit_out(kb,Pf): emit(kb,state['panel'],Pf)
    p32=packed(0,0)
    for kb in range(8):
        if kb==0: pending.append(functools.partial(prep,0))
        P=[p32[8*r:8*r+8,:] for r in range(4)]
        P,V=eliminate(P,lane,row,tick)
        while pending: pending.pop(0)()
        Pf=jnp.concatenate(P,0); Vf=jnp.concatenate(V,0)
        if kb<7:
            rn=mms(lstack(Vf),state['q'])
            h,l=split(rn)
            G=dg(jnp.concatenate([h,h,l],0),jnp.concatenate([h,l,h],0),((0,),(0,)))
            g=G[0:32,:]
            for t in range(1,4): g=jnp.where(grp32==t,G[32*t:32*t+32,:],g)
            p32=state['d']-g
        pending.append(functools.partial(make_panel,kb,Vf))
        for i in range(kb+1,8):
            pending.append(functools.partial(go,i,32*kb))
            if i==min(kb+2,7) and kb+1<7: pending.append(functools.partial(prep,kb+1))
        pending.append(functools.partial(emit_out,kb,Pf))
    while pending: pending.pop(0)()
    r_ref[...]=Rb[0]
    for t in range(3):
        tr_ref[t]=mmt(Rb[t],Wb[t]).astype(jnp.bfloat16)

def factor_all(seg_gram, mine, other):
    return pl.pallas_call(
        factor_kernel,
        out_shape=(
            jax.ShapeDtypeStruct((256, 256), jnp.float32),
            jax.ShapeDtypeStruct((LEVELS, 256, 256), jnp.bfloat16),
        ),
        in_specs=[VMEM] * 3,
        out_specs=[VMEM] * 2,
        scratch_shapes=[
            pltpu.VMEM((8, 128, 256), jnp.float32),
            pltpu.VMEM((4, 256, 256), jnp.float32),
            pltpu.VMEM((3, 256, 256), jnp.float32),
        ],
        compiler_params=params(),
    )(seg_gram, mine, other)


def body(
    near_blocks, sample_cols, near_list, row_basis_t, col_basis_t, couplings, far_source, far_dest
):
    leaf_count, near_count, leaf_rows, _ = near_blocks.shape
    width = sample_cols.shape[1]
    rank = row_basis_t.shape[1]
    n_seg, n_sub = lax.axis_size("seg"), lax.axis_size("sub")
    n = n_seg * n_sub
    rows = leaf_count * leaf_rows

    swap = lax.ppermute(sample_cols, AXES, [(i, i ^ 1) for i in range(n)])
    ahead = [(i, i + 1) for i in range(1, n - 1, 2)]
    cross = lax.ppermute(sample_cols, AXES, ahead + [(j, i) for i, j in ahead])

    slots = far_source.shape[3]
    basis_first, swap = lax.optimization_barrier((col_basis_t, swap))
    high = n_seg // PLANE
    hbm = pl.BlockSpec(memory_space=pltpu.HBM)
    bf16 = jnp.bfloat16
    mine, row_basis, *pays = pl.pallas_call(
        first_kernel,
        out_shape=[
            jax.ShapeDtypeStruct((1, leaf_count * rank + 8, width), bf16),
            jax.ShapeDtypeStruct(row_basis_t.shape, bf16),
        ]
        + [jax.ShapeDtypeStruct((1, high * rank + 8, slots * rank), bf16)] * PLANE,
        in_specs=[hbm] * 4 + [VMEM] * 2,
        out_specs=[VMEM] * (2 + PLANE),
        scratch_shapes=[
            pltpu.VMEM(col_basis_t.shape, bf16),
            pltpu.VMEM(sample_cols.shape, bf16),
            pltpu.VMEM(couplings.shape[2:], bf16),
            pltpu.VMEM((2, 8, 256), jnp.float32),
            pltpu.SemaphoreType.DMA((4,)),
        ],
        compiler_params=params(FIRST_KIB),
    )(
        basis_first,
        sample_cols,
        couplings,
        row_basis_t,
        jnp.swapaxes(far_source[0, 0], 0, 1),
        jnp.swapaxes(far_dest[0, 0], 0, 1),
    )

    column = [hop(mine, PLANE * k, PLANE * k) for k in range(1, high)]
    gathered = [hop(pays[m], m, m) for m in range(1, PLANE)]
    near_part = pl.pallas_call(
        near_kernel,
        out_shape=jax.ShapeDtypeStruct((rows, width), jnp.float32),
        in_specs=[hbm, VMEM, hbm, VMEM, VMEM],
        out_specs=VMEM,
        scratch_shapes=[
            pltpu.VMEM((3 * leaf_count + 1, leaf_rows, width), bf16),
            pltpu.SMEM(near_list.shape, jnp.int32),
            pltpu.SemaphoreType.DMA((1 + leaf_count,)),
        ],
        compiler_params=params(NEAR_KIB),
        cost_estimate=pl.CostEstimate(
            flops=2 * rows * near_count * leaf_rows * width,
            bytes_accessed=near_blocks.size * 2 + 5 * rows * width * 2,
            transcendentals=0,
        ),
    )(near_list, near_blocks, sample_cols, swap, cross)
    column, gathered, near_part = lax.optimization_barrier((column, gathered, near_part))
    own, *parts = pl.pallas_call(
        functools.partial(partial_kernel, leaf_count, slots),
        out_shape=[jax.ShapeDtypeStruct((1, leaf_count * rank, width), jnp.float32)]
        + [jax.ShapeDtypeStruct((1, leaf_count * rank, width), bf16)] * (PLANE - 1),
        in_specs=[VMEM] * (PLANE + high),
        out_specs=[VMEM] * PLANE,
        compiler_params=params(),
    )(mine, *column, pays[0], *gathered)
    got = [hop(parts[m - 1], m, m) for m in range(1, PLANE)]

    samples, gram = pl.pallas_call(
        combine_kernel,
        out_shape=(
            jax.ShapeDtypeStruct((rows, width), jnp.bfloat16),
            jax.ShapeDtypeStruct((320, 128), jnp.float32),
        ),
        in_specs=[VMEM] * (3 + PLANE - 1),
        out_specs=[VMEM] * 2,
        compiler_params=params(),
    )(row_basis, near_part, own, *got)

    total, mask = gram, 1
    while mask < n_sub:
        total = total + sub_hop(total, mask)
        mask *= 2
    seg_gram = total / (n_sub * rows)
    rounded = seg_gram.astype(jnp.bfloat16)
    near = [
        hop(rounded, *masks).astype(jnp.float32) for masks in ((1, 4), (2, 6), (3, 5), (None, 7))
    ]
    odd = (lax.axis_index("sub") % 2) == 1
    pair = seg_gram + near[0]
    quad = (near[1] + near[2]) + pair
    far_quad = (near[0] + near[1]) + (near[2] + near[3])
    sent = jnp.stack([jnp.where(odd, far_quad * 0.25, pair * 0.5), quad * 0.25])
    received = sub_hop(sent, 1)
    segment_factor, transfers = factor_all(seg_gram, sent, received)
    return (samples, segment_factor, transfers[None])


def solution(mesh):
    in_specs = (
        P(("seg", "sub"), None, None, None),
        P(("seg", "sub"), None),
        P(("seg", "sub"), None),
        P(("seg", "sub"), None, None),
        P(("seg", "sub"), None, None),
        P("seg", "sub", None, None, None),
        P("seg", "sub", None, None),
        P("seg", "sub", None, None),
    )
    out_specs = (P(("seg", "sub"), None), P("seg", None), P("seg", None, None, None))
    return jax.shard_map(body, mesh=mesh, in_specs=in_specs, out_specs=out_specs, check_vma=False)
```

```python
import functools

import jax
import jax.numpy as jnp
from jax import lax
from jax.experimental import pallas as pl
from jax.experimental.pallas import tpu as pltpu
from jax.sharding import PartitionSpec as P

LEVELS = 3
PLANE = 4
NEAR_KIB = 49152
FIRST_KIB = 61440
AXES = ("seg", "sub")
VMEM = pl.BlockSpec(memory_space=pltpu.VMEM)
SMEM = pl.BlockSpec(memory_space=pltpu.SMEM)


def params(kib=48 * 2**10):
    return pltpu.CompilerParams(vmem_limit_bytes=kib * 2**10)


def hop(value, even, odd):
    n_seg, n_sub = lax.axis_size("seg"), lax.axis_size("sub")
    pairs = []
    for s in range(n_seg):
        for u in range(n_sub):
            mask = odd if u % 2 else even
            if mask:
                pairs.append((s * n_sub + u, (s ^ mask) * n_sub + u))
    return lax.ppermute(value, AXES, pairs)


def sub_hop(value, mask):
    return lax.ppermute(value, "sub", [(i, i ^ mask) for i in range(lax.axis_size("sub"))])


def pack(top, low):
    lane = lax.broadcasted_iota(jnp.int32, (64, 128), 1)
    corner = pltpu.roll(low[64:128, :], 64, 1)
    mixed = jnp.where(lane < 64, corner, top[64:128, 0:128])
    return jnp.concatenate([top[0:64, 0:128], mixed, top[:, 128:256], low[0:64, :]], 0)


def unpack(packed):
    zero = jnp.zeros((64, 128), jnp.float32)
    left = jnp.concatenate([packed[0:128, :], zero, zero], 0)
    right = jnp.concatenate(
        [packed[128:256, :], packed[256:320, :], pltpu.roll(packed[64:128, :], 64, 1)], 0
    )
    return jnp.concatenate([left, right], 1)


def dot(a, b):
    return jnp.dot(a, b, preferred_element_type=jnp.float32)


def dot_t(a, b):
    return lax.dot_general(a, b, (((0,), (0,)), ((), ())), preferred_element_type=jnp.float32)


def first_kernel(basis_hbm, cols_hbm, couplings_hbm, row_hbm, source_ref, dest_ref, *rest):
    mine_ref, row_ref, *pay_refs, basis, cols, couplings, flags, sems = rest
    copies = [
        pltpu.make_async_copy(src, dst, sems.at[i])
        for i, (src, dst) in enumerate(
            ((basis_hbm, basis), (cols_hbm, cols), (couplings_hbm.at[0, 0], couplings), (row_hbm, row_ref))
        )
    ]
    for copy in copies:
        copy.start()
    slots, peers = source_ref.shape
    leaves, rank, rows = basis.shape
    for i, ref in enumerate((source_ref, dest_ref)):
        flags[i] = jnp.zeros(flags.shape[1:], jnp.float32)
        flags[i, 0:slots, 0:peers] = ref[...].astype(jnp.float32)
    copies[0].wait()
    copies[1].wait()
    for l in range(leaves):
        mine_ref[0, l * rank : (l + 1) * rank, :] = dot(
            basis[l], cols[l * rows : (l + 1) * rows, :]
        ).astype(jnp.bfloat16)
    mine_ref[0, leaves * rank : leaves * rank + 8, :] = flags[0].astype(jnp.bfloat16)
    copies[2].wait()
    copies[3].wait()
    me = lax.axis_index("seg")
    high = peers // PLANE
    for m, pay in enumerate(pay_refs):
        for z in range(high):
            pay[0, z * rank : (z + 1) * rank, :] = couplings[z * PLANE + (me ^ m) % PLANE]
        pay[0, high * rank : high * rank + 8, :] = flags[1, :, 0:128].astype(jnp.bfloat16)


def partial_kernel(leaves, slots, *refs):
    high = len(refs) - 2 * PLANE
    blocks, couplings, outs = refs[:high], refs[high : high + PLANE], refs[high + PLANE :]
    rank = (blocks[0].shape[1] - 8) // leaves
    me = lax.axis_index("seg")
    lane8 = lax.broadcasted_iota(jnp.int32, (8, 128), 1)
    lane = lax.broadcasted_iota(jnp.int32, (1, slots * rank), 1)

    def pick(flags, index):
        return jnp.sum(jnp.where(lane8 == index, flags, 0.0), axis=1, keepdims=True)

    sources = [ref[0, leaves * rank : leaves * rank + 8, 0:128].astype(jnp.float32) for ref in blocks]
    for m in range(PLANE):
        target = me ^ m
        dests = couplings[m][0, high * rank : high * rank + 8, :].astype(jnp.float32)
        total = jnp.zeros((leaves * rank, 256), jnp.float32)
        for k in range(high):
            source = pick(sources[k], target)
            dest = pick(dests, me ^ (PLANE * k))
            chosen = []
            for c in range(slots):
                flag = jnp.broadcast_to(source[c : c + 1, :], (1, 256))
                chosen.append(
                    sum(
                        blocks[k][0, y * rank : (y + 1) * rank, :]
                        * jnp.where(flag == y, 1.0, 0.0).astype(jnp.bfloat16)
                        for y in range(leaves)
                    )
                )
            at = pl.multiple_of(((me // PLANE) ^ k) * rank, rank)
            matrix = couplings[m][0, pl.ds(at, rank), :]
            wide = jnp.broadcast_to(dest[0:1, :], lane.shape)
            for c in range(1, slots):
                wide = jnp.where(lane >= c * rank, dest[c : c + 1, :], wide)
            routed = [
                matrix * jnp.where(wide == l, 1.0, 0.0).astype(jnp.bfloat16) for l in range(leaves)
            ]
            total = total + dot(jnp.concatenate(routed, 0), jnp.concatenate(chosen, 0))
        outs[m][0] = total.astype(outs[m].dtype)


def near_kernel(list_hbm, blocks_ref, own_hbm, swap_ref, cross_ref, out_ref, held, entries, sems):
    leaves, count, rows, _ = blocks_ref.shape
    pairs = [(list_hbm, entries)]
    pairs += [(own_hbm.at[pl.ds(j * rows, rows)], held.at[j]) for j in range(leaves)]
    copies = [pltpu.make_async_copy(src, dst, sems.at[i]) for i, (src, dst) in enumerate(pairs)]
    for copy in copies:
        copy.start()
    for i, src in enumerate((swap_ref, cross_ref)):
        for j in range(leaves):
            held[(i + 1) * leaves + j] = src[j * rows : (j + 1) * rows, :]
    held[3 * leaves] = jnp.zeros(held.shape[1:], held.dtype)
    for copy in copies:
        copy.wait()
    device = lax.axis_index("seg") * lax.axis_size("sub") + lax.axis_index("sub")
    odd = device % 2
    before = (2 - odd) * leaves
    after = (1 + odd) * leaves
    for l in range(leaves):
        acc = jnp.zeros((rows, held.shape[2]), jnp.float32)
        for k in range(count):
            entry = entries[l, k]
            shift = entry - device * leaves
            outside = jnp.where(shift < 0, before + leaves + shift, after + shift - leaves)
            slot = jnp.where((shift < 0) | (shift >= leaves), outside, shift)
            slot = jnp.where(entry < 0, 3 * leaves, slot)
            acc = acc + dot(blocks_ref[l, k], held[slot])
        out_ref[l * rows : (l + 1) * rows, :] = acc


def combine_kernel(basis_ref, near_ref, own_ref, *refs):
    *got, samples_ref, gram_ref = refs
    leaves, rank, rows = basis_ref.shape
    total = own_ref[0]
    for ref in got:
        total = total + ref[0].astype(jnp.float32)
    coeff = total.astype(jnp.bfloat16)
    for l in range(leaves):
        far = dot_t(basis_ref[l], coeff[l * rank : (l + 1) * rank, :])
        at = slice(l * rows, (l + 1) * rows)
        samples_ref[at, :] = (near_ref[at, :] + far).astype(jnp.bfloat16)
    left, right = samples_ref[:, 0:128], samples_ref[:, 128:256]
    top = dot_t(left, samples_ref[...])
    gram_ref[...] = pack(top, dot_t(right, right))


def rb(x,k): return jnp.broadcast_to(x[k:k+1,:],(8,128))

def split(a):
    h=a.astype(jnp.bfloat16); return h,(a-h.astype(jnp.float32)).astype(jnp.bfloat16)
def dg(a,b,dims): return lax.dot_general(a,b,(dims,((),())),preferred_element_type=jnp.float32)
def lstack(a):
    h,l=split(a); return jnp.concatenate([h,l,h],1)
def rstack(b):
    h,l=split(b); return jnp.concatenate([h,h,l],0)
def mms(a,b): return dg(a,b,((1,),(0,)))
def mmt(a,b):
    ah,al=split(a); bh,bl=split(b)
    return dg(jnp.concatenate([ah,al,ah],1),jnp.concatenate([bh,bh,bl],1),((1,),(1,)))
def eliminate(P, Q, lane, row, tick):
    base=lane & ~31
    sub=lane & 31
    V=[jnp.where(row+8*rv==sub,1.0,0.0).astype(jnp.float32) for rv in range(4)]
    P=list(P)
    late=[]
    def follow(r,Ms,rs):
        for k in range(8):
            fq=rb(Q[r],k)
            for rv in range(r,4):
                Q[rv]=Q[rv]-Ms[k][rv]*fq
        Q[r]=Q[r]*rs
    W=16//8
    for mb in range(32//16):
        base_r=mb*W
        C=[{rv:jnp.take_along_axis(P[rv],base+(16*mb+k),axis=1,mode="promise_in_bounds") for rv in range(base_r,4)} for k in range(16)]
        for w in range(W):
            r=base_r+w
            piv=jnp.ones((8,128),jnp.float32)
            Ms=[]
            for kk in range(8):
                k=8*w+kk
                d=rb(C[k][r],kk)
                piv=jnp.where(row==kk,d,piv)
                inv=1.0/d
                nxt=None
                if k+1<16:
                    r1=base_r+(k+1)//8
                    f1=rb(C[k+1][r],kk)
                    t1=C[k][r1]*f1
                    if r1==r: t1=jnp.where(row>kk,t1,0.0)
                    nxt=C[k+1][r1]-t1*inv
                M={rv:C[k][rv]*inv for rv in range(r,4)}
                M[r]=jnp.where(row>kk,M[r],0.0)
                Ms.append(M)
                for k2 in range(k+1,16):
                    f=rb(C[k2][r],kk)
                    for rv in range(r,4):
                        if rv>=base_r+k2//8 or True: C[k2][rv]=C[k2][rv]-M[rv]*f
                if nxt is not None: C[k+1][r1]=nxt
                fp=rb(P[r],kk); fv=rb(V[r],kk)
                for rv in range(r,4):
                    P[rv]=P[rv]-M[rv]*fp
                    V[rv]=V[rv]-M[rv]*fv
                tick(8*r+kk)
            rs=lax.rsqrt(piv)
            P[r]=P[r]*rs
            V[r]=V[r]*rs
            late.append((r,Ms,rs))
            if Q is not None and r>=1: follow(*late[r-1])
    if Q is not None: follow(*late[3])
    return P,V,Q

def factor_kernel(seg_ref, mine_ref, other_ref, r_ref, tr_ref, X, Rb, Wb):
    lane=lax.broadcasted_iota(jnp.int32,(8,128),1); row=lax.broadcasted_iota(jnp.int32,(8,128),0)
    grp=lane//32
    l32=lax.broadcasted_iota(jnp.int32,(32,256),1)
    r32=lax.broadcasted_iota(jnp.int32,(32,256),0)
    bd=(lax.broadcasted_iota(jnp.int32,(128,128),0)//32)==(lax.broadcasted_iota(jnp.int32,(128,128),1)//32)
    l256=lax.broadcasted_iota(jnp.int32,(128,256),1); r256=lax.broadcasted_iota(jnp.int32,(128,256),0)&31
    odd = (lax.axis_index("sub") % 2) == 1
    mine, other = mine_ref[...], other_ref[...]
    first = jnp.where(odd, other, mine)
    second = jnp.where(odd, mine[0], other[0])
    levels = [seg_ref[...], first[0], first[1], (first[1] + second) * 0.5]
    for t, packed in enumerate(levels):
        rows = unpack(packed)
        for kb in range(8):
            X[kb, 32 * t : 32 * t + 32, :] = rows[32 * kb : 32 * kb + 32, :]
    pending=[]
    def tick(step):
        if pending and step%2==2-1: pending.pop(0)()
    def update(i,L,ps,off):
        X[i]=jnp.where((l256>=off)&(l256<off+32),0.0,X[i])-mms(L,ps)
    def emit(kb,panel,Pf):
        off=32*kb; lo=off%128
        for t in range(4):
            pt=panel[32*t:32*t+32,:]
            sh=(lo-32*t)%128
            d=Pf
            if sh: d=pltpu.roll(d,sh,1)
            d2=jnp.concatenate([d,d],1)
            Rb[t,off:off+32,:]=jnp.where(l32>=off+32,pt,jnp.where((l32>=off)&(l32-off>=r32),d2,0.0))
            if t>0: Wb[t-1,off:off+32,:]=jnp.where(l32<off+32,pt,0.0)
    def place(rows_of, block, lo):
        out=[]
        for t in range(4):
            sh=(32*t-lo)%128
            v=rows_of(t)
            out.append(pltpu.roll(v,sh,1) if sh else v)
        return out
    grp32=lax.broadcasted_iota(jnp.int32,(32,128),1)//32
    state={}
    def placed(block, cb):
        off=32*cb; c0=off//128*128
        return place(lambda t:X[block,32*t:32*t+32,c0:c0+128],block,off%128)
    def pick(vs):
        acc=vs[0]
        for t in range(1,4): acc=jnp.where(grp32==t,vs[t],acc)
        return acc
    def prep(kb):
        state['d']=pick(placed(kb+1,kb+1))
        if kb+2<8:
            state['q2']=rstack(jnp.where(bd,jnp.concatenate(placed(kb,kb+2),0),0.0))
            state['qpre']=pick(placed(kb+1,kb+2))
    def rows(x): return [x[8*r:8*r+8,:] for r in range(4)]
    def make_panel(kb,Vf):
        off=32*kb
        Wbd=jnp.where(bd,jnp.concatenate([Vf]*4,0),0.0)
        x=X[kb]
        x=jnp.where((l256>=off)&(l256<off+32),jnp.where(l256-off==r256,1.0,0.0),x)
        state['panel']=mms(lstack(Wbd),rstack(x))
        state['ps']=rstack(state['panel'])
        state['ch']={}
    def go(i,off):
        c=i//4
        if c not in state['ch']: state['ch'][c]=jnp.transpose(state['panel'][:,c*128:c*128+128])
        T=state['ch'][c][(i%4)*32:(i%4)*32+32,:]
        update(i,lstack(jnp.where(bd,jnp.concatenate([T]*4,0),0.0)),state['ps'],off)
    def emit_out(kb,Pf): emit(kb,state['panel'],Pf)
    p32=pick(placed(0,0)); q32=pick(placed(0,1))
    for kb in range(8):
        if kb==0: pending.append(functools.partial(prep,0))
        P,V,Q=eliminate(rows(p32),rows(q32) if kb<7 else None,lane,row,tick)
        while pending: pending.pop(0)()
        Pf=jnp.concatenate(P,0); Vf=jnp.concatenate(V,0)
        if kb<7:
            h,l=split(jnp.concatenate(Q,0))
            left=jnp.concatenate([h,h,l],0)
            G=dg(left,jnp.concatenate([h,l,h],0),((0,),(0,)))
            p32=state['d']-pick([G[32*t:32*t+32,:] for t in range(4)])
            if kb+2<8:
                h2,l2=split(mms(lstack(Vf),state['q2']))
                G2=dg(left,jnp.concatenate([h2,l2,h2],0),((0,),(0,)))
                q32=state['qpre']-pick([G2[32*t:32*t+32,:] for t in range(4)])
        pending.append(functools.partial(make_panel,kb,Vf))
        for i in range(kb+1,8):
            pending.append(functools.partial(go,i,32*kb))
            if i==min(kb+2,7) and kb+1<7: pending.append(functools.partial(prep,kb+1))
        pending.append(functools.partial(emit_out,kb,Pf))
    while pending: pending.pop(0)()
    r_ref[...]=Rb[0]
    for t in range(3):
        tr_ref[t]=mmt(Rb[t],Wb[t]).astype(jnp.bfloat16)

def factor_all(seg_gram, mine, other):
    return pl.pallas_call(
        factor_kernel,
        out_shape=(
            jax.ShapeDtypeStruct((256, 256), jnp.float32),
            jax.ShapeDtypeStruct((LEVELS, 256, 256), jnp.bfloat16),
        ),
        in_specs=[VMEM] * 3,
        out_specs=[VMEM] * 2,
        scratch_shapes=[
            pltpu.VMEM((8, 128, 256), jnp.float32),
            pltpu.VMEM((4, 256, 256), jnp.float32),
            pltpu.VMEM((3, 256, 256), jnp.float32),
        ],
        compiler_params=params(),
    )(seg_gram, mine, other)


def body(
    near_blocks, sample_cols, near_list, row_basis_t, col_basis_t, couplings, far_source, far_dest
):
    leaf_count, near_count, leaf_rows, _ = near_blocks.shape
    width = sample_cols.shape[1]
    rank = row_basis_t.shape[1]
    n_seg, n_sub = lax.axis_size("seg"), lax.axis_size("sub")
    n = n_seg * n_sub
    rows = leaf_count * leaf_rows

    swap = lax.ppermute(sample_cols, AXES, [(i, i ^ 1) for i in range(n)])
    ahead = [(i, i + 1) for i in range(1, n - 1, 2)]
    cross = lax.ppermute(sample_cols, AXES, ahead + [(j, i) for i, j in ahead])

    slots = far_source.shape[3]
    basis_first, swap = lax.optimization_barrier((col_basis_t, swap))
    high = n_seg // PLANE
    hbm = pl.BlockSpec(memory_space=pltpu.HBM)
    bf16 = jnp.bfloat16
    mine, row_basis, *pays = pl.pallas_call(
        first_kernel,
        out_shape=[
            jax.ShapeDtypeStruct((1, leaf_count * rank + 8, width), bf16),
            jax.ShapeDtypeStruct(row_basis_t.shape, bf16),
        ]
        + [jax.ShapeDtypeStruct((1, high * rank + 8, slots * rank), bf16)] * PLANE,
        in_specs=[hbm] * 4 + [VMEM] * 2,
        out_specs=[VMEM] * (2 + PLANE),
        scratch_shapes=[
            pltpu.VMEM(col_basis_t.shape, bf16),
            pltpu.VMEM(sample_cols.shape, bf16),
            pltpu.VMEM(couplings.shape[2:], bf16),
            pltpu.VMEM((2, 8, 256), jnp.float32),
            pltpu.SemaphoreType.DMA((4,)),
        ],
        compiler_params=params(FIRST_KIB),
    )(
        basis_first,
        sample_cols,
        couplings,
        row_basis_t,
        jnp.swapaxes(far_source[0, 0], 0, 1),
        jnp.swapaxes(far_dest[0, 0], 0, 1),
    )

    column = [hop(mine, PLANE * k, PLANE * k) for k in range(1, high)]
    gathered = [hop(pays[m], m, m) for m in range(1, PLANE)]
    near_part = pl.pallas_call(
        near_kernel,
        out_shape=jax.ShapeDtypeStruct((rows, width), jnp.float32),
        in_specs=[hbm, VMEM, hbm, VMEM, VMEM],
        out_specs=VMEM,
        scratch_shapes=[
            pltpu.VMEM((3 * leaf_count + 1, leaf_rows, width), bf16),
            pltpu.SMEM(near_list.shape, jnp.int32),
            pltpu.SemaphoreType.DMA((1 + leaf_count,)),
        ],
        compiler_params=params(NEAR_KIB),
        cost_estimate=pl.CostEstimate(
            flops=2 * rows * near_count * leaf_rows * width,
            bytes_accessed=near_blocks.size * 2 + 5 * rows * width * 2,
            transcendentals=0,
        ),
    )(near_list, near_blocks, sample_cols, swap, cross)
    column, gathered, near_part = lax.optimization_barrier((column, gathered, near_part))
    own, *parts = pl.pallas_call(
        functools.partial(partial_kernel, leaf_count, slots),
        out_shape=[jax.ShapeDtypeStruct((1, leaf_count * rank, width), jnp.float32)]
        + [jax.ShapeDtypeStruct((1, leaf_count * rank, width), bf16)] * (PLANE - 1),
        in_specs=[VMEM] * (PLANE + high),
        out_specs=[VMEM] * PLANE,
        compiler_params=params(),
    )(mine, *column, pays[0], *gathered)
    got = [hop(parts[m - 1], m, m) for m in range(1, PLANE)]

    samples, gram = pl.pallas_call(
        combine_kernel,
        out_shape=(
            jax.ShapeDtypeStruct((rows, width), jnp.bfloat16),
            jax.ShapeDtypeStruct((320, 128), jnp.float32),
        ),
        in_specs=[VMEM] * (3 + PLANE - 1),
        out_specs=[VMEM] * 2,
        compiler_params=params(),
    )(row_basis, near_part, own, *got)

    total, mask = gram, 1
    while mask < n_sub:
        total = total + sub_hop(total, mask)
        mask *= 2
    seg_gram = total / (n_sub * rows)
    rounded = seg_gram.astype(jnp.bfloat16)
    near = [
        hop(rounded, *masks).astype(jnp.float32) for masks in ((1, 4), (2, 6), (3, 5), (None, 7))
    ]
    odd = (lax.axis_index("sub") % 2) == 1
    pair = seg_gram + near[0]
    quad = (near[1] + near[2]) + pair
    far_quad = (near[0] + near[1]) + (near[2] + near[3])
    sent = jnp.stack([jnp.where(odd, far_quad * 0.25, pair * 0.5), quad * 0.25])
    received = sub_hop(sent, 1)
    segment_factor, transfers = factor_all(seg_gram, sent, received)
    return (samples, segment_factor, transfers[None])


def solution(mesh):
    in_specs = (
        P(("seg", "sub"), None, None, None),
        P(("seg", "sub"), None),
        P(("seg", "sub"), None),
        P(("seg", "sub"), None, None),
        P(("seg", "sub"), None, None),
        P("seg", "sub", None, None, None),
        P("seg", "sub", None, None),
        P("seg", "sub", None, None),
    )
    out_specs = (P(("seg", "sub"), None), P("seg", None), P("seg", None, None, None))
    return jax.shard_map(body, mesh=mesh, in_specs=in_specs, out_specs=out_specs, check_vma=False)
```

```python
import functools

import jax
import jax.numpy as jnp
from jax import lax
from jax.experimental import pallas as pl
from jax.experimental.pallas import tpu as pltpu
from jax.sharding import PartitionSpec as P

LEVELS = 3
PLANE = 4
NEAR_KIB = 49152
FIRST_KIB = 61440
AXES = ("seg", "sub")
VMEM = pl.BlockSpec(memory_space=pltpu.VMEM)
SMEM = pl.BlockSpec(memory_space=pltpu.SMEM)


def params(kib=48 * 2**10):
    return pltpu.CompilerParams(vmem_limit_bytes=kib * 2**10)


def hop(value, even, odd):
    n_seg, n_sub = lax.axis_size("seg"), lax.axis_size("sub")
    pairs = []
    for s in range(n_seg):
        for u in range(n_sub):
            mask = odd if u % 2 else even
            if mask:
                pairs.append((s * n_sub + u, (s ^ mask) * n_sub + u))
    return lax.ppermute(value, AXES, pairs)


def sub_hop(value, mask):
    return lax.ppermute(value, "sub", [(i, i ^ mask) for i in range(lax.axis_size("sub"))])


def pack(top, low):
    lane = lax.broadcasted_iota(jnp.int32, (64, 128), 1)
    corner = pltpu.roll(low[64:128, :], 64, 1)
    mixed = jnp.where(lane < 64, corner, top[64:128, 0:128])
    return jnp.concatenate([top[0:64, 0:128], mixed, top[:, 128:256], low[0:64, :]], 0)


def unpack(packed):
    zero = jnp.zeros((64, 128), jnp.float32)
    left = jnp.concatenate([packed[0:128, :], zero, zero], 0)
    right = jnp.concatenate(
        [packed[128:256, :], packed[256:320, :], pltpu.roll(packed[64:128, :], 64, 1)], 0
    )
    return jnp.concatenate([left, right], 1)


def dot(a, b):
    return jnp.dot(a, b, preferred_element_type=jnp.float32)


def dot_t(a, b):
    return lax.dot_general(a, b, (((0,), (0,)), ((), ())), preferred_element_type=jnp.float32)


def first_kernel(basis_hbm, cols_hbm, couplings_hbm, row_hbm, source_ref, dest_ref, *rest):
    mine_ref, row_ref, *pay_refs, basis, cols, couplings, flags, sems = rest
    copies = [
        pltpu.make_async_copy(src, dst, sems.at[i])
        for i, (src, dst) in enumerate(
            ((basis_hbm, basis), (cols_hbm, cols), (couplings_hbm.at[0, 0], couplings), (row_hbm, row_ref))
        )
    ]
    for copy in copies:
        copy.start()
    slots, peers = source_ref.shape
    leaves, rank, rows = basis.shape
    for i, ref in enumerate((source_ref, dest_ref)):
        flags[i] = jnp.zeros(flags.shape[1:], jnp.float32)
        flags[i, 0:slots, 0:peers] = ref[...].astype(jnp.float32)
    copies[0].wait()
    copies[1].wait()
    for l in range(leaves):
        mine_ref[0, l * rank : (l + 1) * rank, :] = dot(
            basis[l], cols[l * rows : (l + 1) * rows, :]
        ).astype(jnp.bfloat16)
    mine_ref[0, leaves * rank : leaves * rank + 8, :] = flags[0].astype(jnp.bfloat16)
    copies[2].wait()
    copies[3].wait()
    me = lax.axis_index("seg")
    high = peers // PLANE
    for m, pay in enumerate(pay_refs):
        for z in range(high):
            pay[0, z * rank : (z + 1) * rank, :] = couplings[z * PLANE + (me ^ m) % PLANE]
        pay[0, high * rank : high * rank + 8, :] = flags[1, :, 0:128].astype(jnp.bfloat16)


def partial_kernel(leaves, slots, *refs):
    high = len(refs) - 2 * PLANE
    blocks, couplings, outs = refs[:high], refs[high : high + PLANE], refs[high + PLANE :]
    rank = (blocks[0].shape[1] - 8) // leaves
    me = lax.axis_index("seg")
    lane8 = lax.broadcasted_iota(jnp.int32, (8, 128), 1)
    lane = lax.broadcasted_iota(jnp.int32, (1, slots * rank), 1)

    def pick(flags, index):
        return jnp.sum(jnp.where(lane8 == index, flags, 0.0), axis=1, keepdims=True)

    sources = [ref[0, leaves * rank : leaves * rank + 8, 0:128].astype(jnp.float32) for ref in blocks]
    for m in range(PLANE):
        target = me ^ m
        dests = couplings[m][0, high * rank : high * rank + 8, :].astype(jnp.float32)
        total = jnp.zeros((leaves * rank, 256), jnp.float32)
        for k in range(high):
            source = pick(sources[k], target)
            dest = pick(dests, me ^ (PLANE * k))
            chosen = []
            for c in range(slots):
                flag = jnp.broadcast_to(source[c : c + 1, :], (1, 256))
                chosen.append(
                    sum(
                        blocks[k][0, y * rank : (y + 1) * rank, :]
                        * jnp.where(flag == y, 1.0, 0.0).astype(jnp.bfloat16)
                        for y in range(leaves)
                    )
                )
            at = pl.multiple_of(((me // PLANE) ^ k) * rank, rank)
            matrix = couplings[m][0, pl.ds(at, rank), :]
            wide = jnp.broadcast_to(dest[0:1, :], lane.shape)
            for c in range(1, slots):
                wide = jnp.where(lane >= c * rank, dest[c : c + 1, :], wide)
            routed = [
                matrix * jnp.where(wide == l, 1.0, 0.0).astype(jnp.bfloat16) for l in range(leaves)
            ]
            total = total + dot(jnp.concatenate(routed, 0), jnp.concatenate(chosen, 0))
        outs[m][0] = total.astype(outs[m].dtype)


def near_kernel(leaf, list_hbm, blocks_ref, own_hbm, swap_ref, cross_ref, out_ref, held, entries, sems):
    leaves = entries.shape[0]
    _, count, rows, _ = blocks_ref.shape
    pairs = [(list_hbm, entries)]
    pairs += [(own_hbm.at[pl.ds(j * rows, rows)], held.at[j]) for j in range(leaves)]
    copies = [pltpu.make_async_copy(src, dst, sems.at[i]) for i, (src, dst) in enumerate(pairs)]
    for copy in copies:
        copy.start()
    for i, src in enumerate((swap_ref, cross_ref)):
        for j in range(leaves):
            held[(i + 1) * leaves + j] = src[j * rows : (j + 1) * rows, :]
    held[3 * leaves] = jnp.zeros(held.shape[1:], held.dtype)
    for copy in copies:
        copy.wait()
    device = lax.axis_index("seg") * lax.axis_size("sub") + lax.axis_index("sub")
    odd = device % 2
    before = (2 - odd) * leaves
    after = (1 + odd) * leaves
    acc = jnp.zeros((rows, held.shape[2]), jnp.float32)
    for k in range(count):
        entry = entries[leaf, k]
        shift = entry - device * leaves
        outside = jnp.where(shift < 0, before + leaves + shift, after + shift - leaves)
        slot = jnp.where((shift < 0) | (shift >= leaves), outside, shift)
        slot = jnp.where(entry < 0, 3 * leaves, slot)
        acc = acc + dot(blocks_ref[0, k], held[slot])
    out_ref[...] = acc


def combine_kernel(basis_ref, own_ref, *refs):
    leaves, rank, rows = basis_ref.shape
    nears = refs[:leaves]
    *got, samples_ref, gram_ref = refs[leaves:]
    total = own_ref[0]
    for ref in got:
        total = total + ref[0].astype(jnp.float32)
    coeff = total.astype(jnp.bfloat16)
    for l in range(leaves):
        far = dot_t(basis_ref[l], coeff[l * rank : (l + 1) * rank, :])
        at = slice(l * rows, (l + 1) * rows)
        samples_ref[at, :] = (nears[l][...] + far).astype(jnp.bfloat16)
    left, right = samples_ref[:, 0:128], samples_ref[:, 128:256]
    top = dot_t(left, samples_ref[...])
    gram_ref[...] = pack(top, dot_t(right, right))


def rb(x,k): return jnp.broadcast_to(x[k:k+1,:],(8,128))

def split(a):
    h=a.astype(jnp.bfloat16); return h,(a-h.astype(jnp.float32)).astype(jnp.bfloat16)
def dg(a,b,dims): return lax.dot_general(a,b,(dims,((),())),preferred_element_type=jnp.float32)
def lstack(a):
    h,l=split(a); return jnp.concatenate([h,l,h],1)
def rstack(b):
    h,l=split(b); return jnp.concatenate([h,h,l],0)
def mms(a,b): return dg(a,b,((1,),(0,)))
def mmt(a,b):
    ah,al=split(a); bh,bl=split(b)
    return dg(jnp.concatenate([ah,al,ah],1),jnp.concatenate([bh,bh,bl],1),((1,),(1,)))
def eliminate(P, Q, lane, row, tick):
    base=lane & ~31
    sub=lane & 31
    V=[jnp.where(row+8*rv==sub,1.0,0.0).astype(jnp.float32) for rv in range(4)]
    P=list(P)
    late=[]
    def follow(r,Ms,rs):
        for k in range(8):
            fq=rb(Q[r],k)
            for rv in range(r,4):
                Q[rv]=Q[rv]-Ms[k][rv]*fq
        Q[r]=Q[r]*rs
    W=16//8
    for mb in range(32//16):
        base_r=mb*W
        C=[{rv:jnp.take_along_axis(P[rv],base+(16*mb+k),axis=1,mode="promise_in_bounds") for rv in range(base_r,4)} for k in range(16)]
        for w in range(W):
            r=base_r+w
            piv=jnp.ones((8,128),jnp.float32)
            Ms=[]
            for kk in range(8):
                k=8*w+kk
                d=rb(C[k][r],kk)
                piv=jnp.where(row==kk,d,piv)
                inv=1.0/d
                nxt=None
                if k+1<16:
                    r1=base_r+(k+1)//8
                    f1=rb(C[k+1][r],kk)
                    t1=C[k][r1]*f1
                    if r1==r: t1=jnp.where(row>kk,t1,0.0)
                    nxt=C[k+1][r1]-t1*inv
                M={rv:C[k][rv]*inv for rv in range(r,4)}
                M[r]=jnp.where(row>kk,M[r],0.0)
                Ms.append(M)
                for k2 in range(k+1,16):
                    f=rb(C[k2][r],kk)
                    for rv in range(r,4):
                        if rv>=base_r+k2//8 or True: C[k2][rv]=C[k2][rv]-M[rv]*f
                if nxt is not None: C[k+1][r1]=nxt
                fp=rb(P[r],kk); fv=rb(V[r],kk)
                for rv in range(r,4):
                    P[rv]=P[rv]-M[rv]*fp
                    V[rv]=V[rv]-M[rv]*fv
                tick(8*r+kk)
            rs=lax.rsqrt(piv)
            P[r]=P[r]*rs
            V[r]=V[r]*rs
            late.append((r,Ms,rs))
            if Q is not None and r>=1: follow(*late[r-1])
    if Q is not None: follow(*late[3])
    return P,V,Q

def factor_kernel(seg_ref, mine_ref, other_ref, r_ref, tr_ref, X, Rb, Wb):
    lane=lax.broadcasted_iota(jnp.int32,(8,128),1); row=lax.broadcasted_iota(jnp.int32,(8,128),0)
    grp=lane//32
    l32=lax.broadcasted_iota(jnp.int32,(32,256),1)
    r32=lax.broadcasted_iota(jnp.int32,(32,256),0)
    bd=(lax.broadcasted_iota(jnp.int32,(128,128),0)//32)==(lax.broadcasted_iota(jnp.int32,(128,128),1)//32)
    l256=lax.broadcasted_iota(jnp.int32,(128,256),1); r256=lax.broadcasted_iota(jnp.int32,(128,256),0)&31
    odd = (lax.axis_index("sub") % 2) == 1
    mine, other = mine_ref[...], other_ref[...]
    first = jnp.where(odd, other, mine)
    second = jnp.where(odd, mine[0], other[0])
    levels = [seg_ref[...], first[0], first[1], (first[1] + second) * 0.5]
    for t, packed in enumerate(levels):
        rows = unpack(packed)
        for kb in range(8):
            X[kb, 32 * t : 32 * t + 32, :] = rows[32 * kb : 32 * kb + 32, :]
    pending=[]
    def tick(step):
        if pending and step%2==2-1: pending.pop(0)()
    def update(i,L,ps,off):
        X[i]=jnp.where((l256>=off)&(l256<off+32),0.0,X[i])-mms(L,ps)
    def emit(kb,panel,Pf):
        off=32*kb; lo=off%128
        for t in range(4):
            pt=panel[32*t:32*t+32,:]
            sh=(lo-32*t)%128
            d=Pf
            if sh: d=pltpu.roll(d,sh,1)
            d2=jnp.concatenate([d,d],1)
            Rb[t,off:off+32,:]=jnp.where(l32>=off+32,pt,jnp.where((l32>=off)&(l32-off>=r32),d2,0.0))
            if t>0: Wb[t-1,off:off+32,:]=jnp.where(l32<off+32,pt,0.0)
    def place(rows_of, block, lo):
        out=[]
        for t in range(4):
            sh=(32*t-lo)%128
            v=rows_of(t)
            out.append(pltpu.roll(v,sh,1) if sh else v)
        return out
    grp32=lax.broadcasted_iota(jnp.int32,(32,128),1)//32
    state={}
    def placed(block, cb):
        off=32*cb; c0=off//128*128
        return place(lambda t:X[block,32*t:32*t+32,c0:c0+128],block,off%128)
    def pick(vs):
        acc=vs[0]
        for t in range(1,4): acc=jnp.where(grp32==t,vs[t],acc)
        return acc
    def prep(kb):
        state['d']=pick(placed(kb+1,kb+1))
        if kb+2<8:
            state['q2']=rstack(jnp.where(bd,jnp.concatenate(placed(kb,kb+2),0),0.0))
            state['qpre']=pick(placed(kb+1,kb+2))
    def rows(x): return [x[8*r:8*r+8,:] for r in range(4)]
    def make_panel(kb,Vf):
        off=32*kb
        Wbd=jnp.where(bd,jnp.concatenate([Vf]*4,0),0.0)
        x=X[kb]
        x=jnp.where((l256>=off)&(l256<off+32),jnp.where(l256-off==r256,1.0,0.0),x)
        state['panel']=mms(lstack(Wbd),rstack(x))
        state['ps']=rstack(state['panel'])
        state['ch']={}
    def go(i,off):
        c=i//4
        if c not in state['ch']: state['ch'][c]=jnp.transpose(state['panel'][:,c*128:c*128+128])
        T=state['ch'][c][(i%4)*32:(i%4)*32+32,:]
        update(i,lstack(jnp.where(bd,jnp.concatenate([T]*4,0),0.0)),state['ps'],off)
    def emit_out(kb,Pf): emit(kb,state['panel'],Pf)
    p32=pick(placed(0,0)); q32=pick(placed(0,1))
    for kb in range(8):
        if kb==0: pending.append(functools.partial(prep,0))
        P,V,Q=eliminate(rows(p32),rows(q32) if kb<7 else None,lane,row,tick)
        while pending: pending.pop(0)()
        Pf=jnp.concatenate(P,0); Vf=jnp.concatenate(V,0)
        if kb<7:
            h,l=split(jnp.concatenate(Q,0))
            left=jnp.concatenate([h,h,l],0)
            G=dg(left,jnp.concatenate([h,l,h],0),((0,),(0,)))
            p32=state['d']-pick([G[32*t:32*t+32,:] for t in range(4)])
            if kb+2<8:
                h2,l2=split(mms(lstack(Vf),state['q2']))
                G2=dg(left,jnp.concatenate([h2,l2,h2],0),((0,),(0,)))
                q32=state['qpre']-pick([G2[32*t:32*t+32,:] for t in range(4)])
        pending.append(functools.partial(make_panel,kb,Vf))
        for i in range(kb+1,8):
            pending.append(functools.partial(go,i,32*kb))
            if i==min(kb+2,7) and kb+1<7: pending.append(functools.partial(prep,kb+1))
        pending.append(functools.partial(emit_out,kb,Pf))
    while pending: pending.pop(0)()
    r_ref[...]=Rb[0]
    for t in range(3):
        tr_ref[t]=mmt(Rb[t],Wb[t]).astype(jnp.bfloat16)

def factor_all(seg_gram, mine, other):
    return pl.pallas_call(
        factor_kernel,
        out_shape=(
            jax.ShapeDtypeStruct((256, 256), jnp.float32),
            jax.ShapeDtypeStruct((LEVELS, 256, 256), jnp.bfloat16),
        ),
        in_specs=[VMEM] * 3,
        out_specs=[VMEM] * 2,
        scratch_shapes=[
            pltpu.VMEM((8, 128, 256), jnp.float32),
            pltpu.VMEM((4, 256, 256), jnp.float32),
            pltpu.VMEM((3, 256, 256), jnp.float32),
        ],
        compiler_params=params(),
    )(seg_gram, mine, other)


def body(
    near_blocks, sample_cols, near_list, row_basis_t, col_basis_t, couplings, far_source, far_dest
):
    leaf_count, near_count, leaf_rows, _ = near_blocks.shape
    width = sample_cols.shape[1]
    rank = row_basis_t.shape[1]
    n_seg, n_sub = lax.axis_size("seg"), lax.axis_size("sub")
    n = n_seg * n_sub
    rows = leaf_count * leaf_rows

    swap = lax.ppermute(sample_cols, AXES, [(i, i ^ 1) for i in range(n)])
    ahead = [(i, i + 1) for i in range(1, n - 1, 2)]
    cross = lax.ppermute(sample_cols, AXES, ahead + [(j, i) for i, j in ahead])

    slots = far_source.shape[3]
    basis_first, swap = lax.optimization_barrier((col_basis_t, swap))
    high = n_seg // PLANE
    hbm = pl.BlockSpec(memory_space=pltpu.HBM)
    bf16 = jnp.bfloat16
    mine, row_basis, *pays = pl.pallas_call(
        first_kernel,
        out_shape=[
            jax.ShapeDtypeStruct((1, leaf_count * rank + 8, width), bf16),
            jax.ShapeDtypeStruct(row_basis_t.shape, bf16),
        ]
        + [jax.ShapeDtypeStruct((1, high * rank + 8, slots * rank), bf16)] * PLANE,
        in_specs=[hbm] * 4 + [VMEM] * 2,
        out_specs=[VMEM] * (2 + PLANE),
        scratch_shapes=[
            pltpu.VMEM(col_basis_t.shape, bf16),
            pltpu.VMEM(sample_cols.shape, bf16),
            pltpu.VMEM(couplings.shape[2:], bf16),
            pltpu.VMEM((2, 8, 256), jnp.float32),
            pltpu.SemaphoreType.DMA((4,)),
        ],
        compiler_params=params(FIRST_KIB),
    )(
        basis_first,
        sample_cols,
        couplings,
        row_basis_t,
        jnp.swapaxes(far_source[0, 0], 0, 1),
        jnp.swapaxes(far_dest[0, 0], 0, 1),
    )

    column = [hop(mine, PLANE * k, PLANE * k) for k in range(1, high)]
    gathered = [hop(pays[m], m, m) for m in range(1, PLANE)]
    def near_leaf(leaf):
        return pl.pallas_call(
            functools.partial(near_kernel, leaf),
            out_shape=jax.ShapeDtypeStruct((leaf_rows, width), jnp.float32),
            in_specs=[hbm, VMEM, hbm, VMEM, VMEM],
            out_specs=VMEM,
            scratch_shapes=[
                pltpu.VMEM((3 * leaf_count + 1, leaf_rows, width), bf16),
                pltpu.SMEM(near_list.shape, jnp.int32),
                pltpu.SemaphoreType.DMA((1 + leaf_count,)),
            ],
            compiler_params=params(NEAR_KIB),
            cost_estimate=pl.CostEstimate(
                flops=2 * leaf_rows * near_count * leaf_rows * width,
                bytes_accessed=near_blocks.size + 5 * rows * width * 2,
                transcendentals=0,
            ),
        )(near_list, lax.slice_in_dim(near_blocks, leaf, leaf + 1, axis=0), sample_cols, swap, cross)

    near_parts = [near_leaf(0)]
    column, gathered, near_parts = lax.optimization_barrier((column, gathered, near_parts))
    own, *parts = pl.pallas_call(
        functools.partial(partial_kernel, leaf_count, slots),
        out_shape=[jax.ShapeDtypeStruct((1, leaf_count * rank, width), jnp.float32)]
        + [jax.ShapeDtypeStruct((1, leaf_count * rank, width), bf16)] * (PLANE - 1),
        in_specs=[VMEM] * (PLANE + high),
        out_specs=[VMEM] * PLANE,
        compiler_params=params(),
    )(mine, *column, pays[0], *gathered)
    got = [hop(parts[m - 1], m, m) for m in range(PLANE - 1, 0, -1)]

    near_parts = near_parts + [near_leaf(leaf) for leaf in range(1, leaf_count)]
    samples, gram = pl.pallas_call(
        combine_kernel,
        out_shape=(
            jax.ShapeDtypeStruct((rows, width), jnp.bfloat16),
            jax.ShapeDtypeStruct((320, 128), jnp.float32),
        ),
        in_specs=[VMEM] * (2 + leaf_count + PLANE - 1),
        out_specs=[VMEM] * 2,
        compiler_params=params(),
    )(row_basis, own, *near_parts, *got)

    total, mask = gram, 1
    while mask < n_sub:
        total = total + sub_hop(total, mask)
        mask *= 2
    seg_gram = total / (n_sub * rows)
    rounded = seg_gram.astype(jnp.bfloat16)
    near = [
        hop(rounded, *masks).astype(jnp.float32) for masks in ((1, 4), (2, 6), (3, 5), (None, 7))
    ]
    odd = (lax.axis_index("sub") % 2) == 1
    pair = seg_gram + near[0]
    quad = (near[1] + near[2]) + pair
    far_quad = (near[0] + near[1]) + (near[2] + near[3])
    sent = jnp.stack([jnp.where(odd, far_quad * 0.25, pair * 0.5), quad * 0.25])
    received = sub_hop(sent, 1)
    segment_factor, transfers = factor_all(seg_gram, sent, received)
    return (samples, segment_factor, transfers[None])


def solution(mesh):
    in_specs = (
        P(("seg", "sub"), None, None, None),
        P(("seg", "sub"), None),
        P(("seg", "sub"), None),
        P(("seg", "sub"), None, None),
        P(("seg", "sub"), None, None),
        P("seg", "sub", None, None, None),
        P("seg", "sub", None, None),
        P("seg", "sub", None, None),
    )
    out_specs = (P(("seg", "sub"), None), P("seg", None), P("seg", None, None, None))
    return jax.shard_map(body, mesh=mesh, in_specs=in_specs, out_specs=out_specs, check_vma=False)
```

```python
import functools

import jax
import jax.numpy as jnp
from jax import lax
from jax.experimental import pallas as pl
from jax.experimental.pallas import tpu as pltpu
from jax.sharding import PartitionSpec as P

LEVELS = 3
PLANE = 4
NEAR_KIB = 49152
FIRST_KIB = 61440
AXES = ("seg", "sub")
VMEM = pl.BlockSpec(memory_space=pltpu.VMEM)
SMEM = pl.BlockSpec(memory_space=pltpu.SMEM)


def params(kib=48 * 2**10):
    return pltpu.CompilerParams(vmem_limit_bytes=kib * 2**10)


def hop(value, even, odd):
    n_seg, n_sub = lax.axis_size("seg"), lax.axis_size("sub")
    pairs = []
    for s in range(n_seg):
        for u in range(n_sub):
            mask = odd if u % 2 else even
            if mask:
                pairs.append((s * n_sub + u, (s ^ mask) * n_sub + u))
    return lax.ppermute(value, AXES, pairs)


def sub_hop(value, mask):
    return lax.ppermute(value, "sub", [(i, i ^ mask) for i in range(lax.axis_size("sub"))])


def pack(top, low):
    lane = lax.broadcasted_iota(jnp.int32, (64, 128), 1)
    corner = pltpu.roll(low[64:128, :], 64, 1)
    mixed = jnp.where(lane < 64, corner, top[64:128, 0:128])
    return jnp.concatenate([top[0:64, 0:128], mixed, top[:, 128:256], low[0:64, :]], 0)


def unpack(packed):
    zero = jnp.zeros((64, 128), jnp.float32)
    left = jnp.concatenate([packed[0:128, :], zero, zero], 0)
    right = jnp.concatenate(
        [packed[128:256, :], packed[256:320, :], pltpu.roll(packed[64:128, :], 64, 1)], 0
    )
    return jnp.concatenate([left, right], 1)


def dot(a, b):
    return jnp.dot(a, b, preferred_element_type=jnp.float32)


def dot_t(a, b):
    return lax.dot_general(a, b, (((0,), (0,)), ((), ())), preferred_element_type=jnp.float32)


def first_kernel(basis_hbm, cols_hbm, couplings_hbm, row_hbm, source_ref, dest_ref, *rest):
    mine_ref, row_ref, *pay_refs, basis, cols, couplings, flags, sems = rest
    copies = [
        pltpu.make_async_copy(src, dst, sems.at[i])
        for i, (src, dst) in enumerate(
            ((basis_hbm, basis), (cols_hbm, cols), (couplings_hbm.at[0, 0], couplings), (row_hbm, row_ref))
        )
    ]
    for copy in copies:
        copy.start()
    slots, peers = source_ref.shape
    leaves, rank, rows = basis.shape
    for i, ref in enumerate((source_ref, dest_ref)):
        flags[i] = jnp.zeros(flags.shape[1:], jnp.float32)
        flags[i, 0:slots, 0:peers] = ref[...].astype(jnp.float32)
    copies[0].wait()
    copies[1].wait()
    for l in range(leaves):
        mine_ref[0, l * rank : (l + 1) * rank, :] = dot(
            basis[l], cols[l * rows : (l + 1) * rows, :]
        ).astype(jnp.bfloat16)
    mine_ref[0, leaves * rank : leaves * rank + 8, :] = flags[0].astype(jnp.bfloat16)
    copies[2].wait()
    copies[3].wait()
    me = lax.axis_index("seg")
    high = peers // PLANE
    for m, pay in enumerate(pay_refs):
        for z in range(high):
            pay[0, z * rank : (z + 1) * rank, :] = couplings[z * PLANE + (me ^ m) % PLANE]
        pay[0, high * rank : high * rank + 8, :] = flags[1, :, 0:128].astype(jnp.bfloat16)


def partial_kernel(leaves, slots, *refs):
    high = len(refs) - 2 * PLANE
    blocks, couplings, outs = refs[:high], refs[high : high + PLANE], refs[high + PLANE :]
    rank = (blocks[0].shape[1] - 8) // leaves
    me = lax.axis_index("seg")
    lane8 = lax.broadcasted_iota(jnp.int32, (8, 128), 1)
    lane = lax.broadcasted_iota(jnp.int32, (1, slots * rank), 1)

    def pick(flags, index):
        return jnp.sum(jnp.where(lane8 == index, flags, 0.0), axis=1, keepdims=True)

    sources = [ref[0, leaves * rank : leaves * rank + 8, 0:128].astype(jnp.float32) for ref in blocks]
    for m in range(PLANE):
        target = me ^ m
        dests = couplings[m][0, high * rank : high * rank + 8, :].astype(jnp.float32)
        total = jnp.zeros((leaves * rank, 256), jnp.float32)
        for k in range(high):
            source = pick(sources[k], target)
            dest = pick(dests, me ^ (PLANE * k))
            chosen = []
            for c in range(slots):
                flag = jnp.broadcast_to(source[c : c + 1, :], (1, 256))
                chosen.append(
                    sum(
                        blocks[k][0, y * rank : (y + 1) * rank, :]
                        * jnp.where(flag == y, 1.0, 0.0).astype(jnp.bfloat16)
                        for y in range(leaves)
                    )
                )
            at = pl.multiple_of(((me // PLANE) ^ k) * rank, rank)
            matrix = couplings[m][0, pl.ds(at, rank), :]
            wide = jnp.broadcast_to(dest[0:1, :], lane.shape)
            for c in range(1, slots):
                wide = jnp.where(lane >= c * rank, dest[c : c + 1, :], wide)
            routed = [
                matrix * jnp.where(wide == l, 1.0, 0.0).astype(jnp.bfloat16) for l in range(leaves)
            ]
            total = total + dot(jnp.concatenate(routed, 0), jnp.concatenate(chosen, 0))
        outs[m][0] = total.astype(outs[m].dtype)


def near_kernel(leaf, list_hbm, blocks_ref, own_hbm, swap_ref, cross_ref, out_ref, held, entries, sems):
    leaves = entries.shape[0]
    _, count, rows, _ = blocks_ref.shape
    pairs = [(list_hbm, entries)]
    pairs += [(own_hbm.at[pl.ds(j * rows, rows)], held.at[j]) for j in range(leaves)]
    copies = [pltpu.make_async_copy(src, dst, sems.at[i]) for i, (src, dst) in enumerate(pairs)]
    for copy in copies:
        copy.start()
    for i, src in enumerate((swap_ref, cross_ref)):
        for j in range(leaves):
            held[(i + 1) * leaves + j] = src[j * rows : (j + 1) * rows, :]
    held[3 * leaves] = jnp.zeros(held.shape[1:], held.dtype)
    for copy in copies:
        copy.wait()
    device = lax.axis_index("seg") * lax.axis_size("sub") + lax.axis_index("sub")
    odd = device % 2
    before = (2 - odd) * leaves
    after = (1 + odd) * leaves
    acc = jnp.zeros((rows, held.shape[2]), jnp.float32)
    for k in range(count):
        entry = entries[leaf, k]
        shift = entry - device * leaves
        outside = jnp.where(shift < 0, before + leaves + shift, after + shift - leaves)
        slot = jnp.where((shift < 0) | (shift >= leaves), outside, shift)
        slot = jnp.where(entry < 0, 3 * leaves, slot)
        acc = acc + dot(blocks_ref[0, k], held[slot])
    out_ref[...] = acc


def combine_kernel(basis_ref, own_ref, *refs):
    leaves, rank, rows = basis_ref.shape
    nears = refs[:leaves]
    *got, samples_ref, gram_ref = refs[leaves:]
    total = own_ref[0]
    for ref in got:
        total = total + ref[0].astype(jnp.float32)
    coeff = total.astype(jnp.bfloat16)
    for l in range(leaves):
        far = dot_t(basis_ref[l], coeff[l * rank : (l + 1) * rank, :])
        at = slice(l * rows, (l + 1) * rows)
        samples_ref[at, :] = (nears[l][...] + far).astype(jnp.bfloat16)
    left, right = samples_ref[:, 0:128], samples_ref[:, 128:256]
    top = dot_t(left, samples_ref[...])
    gram_ref[...] = pack(top, dot_t(right, right))


def rb(x,k): return jnp.broadcast_to(x[k:k+1,:],(8,128))

def split(a):
    h=a.astype(jnp.bfloat16); return h,(a-h.astype(jnp.float32)).astype(jnp.bfloat16)
def dg(a,b,dims): return lax.dot_general(a,b,(dims,((),())),preferred_element_type=jnp.float32)
def lstack(a):
    h,l=split(a); return jnp.concatenate([h,l,h],1)
def rstack(b):
    h,l=split(b); return jnp.concatenate([h,h,l],0)
def mms(a,b): return dg(a,b,((1,),(0,)))
def mmt(a,b):
    ah,al=split(a); bh,bl=split(b)
    return dg(jnp.concatenate([ah,al,ah],1),jnp.concatenate([bh,bh,bl],1),((1,),(1,)))
def eliminate(P, Q, lane, row, tick):
    base=lane & ~31
    sub=lane & 31
    V=[jnp.where(row+8*rv==sub,1.0,0.0).astype(jnp.float32) for rv in range(4)]
    P=list(P)
    late=[]
    def follow(r,Ms,rs):
        for k in range(8):
            fq=rb(Q[r],k)
            for rv in range(r,4):
                Q[rv]=Q[rv]-Ms[k][rv]*fq
        Q[r]=Q[r]*rs
    W=16//8
    for mb in range(32//16):
        base_r=mb*W
        C=[{rv:jnp.take_along_axis(P[rv],base+(16*mb+k),axis=1,mode="promise_in_bounds") for rv in range(base_r,4)} for k in range(16)]
        for w in range(W):
            r=base_r+w
            piv=jnp.ones((8,128),jnp.float32)
            Ms=[]
            for kk in range(8):
                k=8*w+kk
                d=rb(C[k][r],kk)
                piv=jnp.where(row==kk,d,piv)
                inv=1.0/d
                nxt=None
                if k+1<16:
                    r1=base_r+(k+1)//8
                    f1=rb(C[k+1][r],kk)
                    t1=C[k][r1]*f1
                    if r1==r: t1=jnp.where(row>kk,t1,0.0)
                    nxt=C[k+1][r1]-t1*inv
                M={rv:C[k][rv]*inv for rv in range(r,4)}
                M[r]=jnp.where(row>kk,M[r],0.0)
                Ms.append(M)
                for k2 in range(k+1,16):
                    f=rb(C[k2][r],kk)
                    for rv in range(r,4):
                        if rv>=base_r+k2//8 or True: C[k2][rv]=C[k2][rv]-M[rv]*f
                if nxt is not None: C[k+1][r1]=nxt
                fp=rb(P[r],kk); fv=rb(V[r],kk)
                for rv in range(r,4):
                    P[rv]=P[rv]-M[rv]*fp
                    V[rv]=V[rv]-M[rv]*fv
                tick(8*r+kk)
            rs=lax.rsqrt(piv)
            P[r]=P[r]*rs
            V[r]=V[r]*rs
            late.append((r,Ms,rs))
            if Q is not None and r>=1: follow(*late[r-1])
    if Q is not None: follow(*late[3])
    return P,V,Q

def factor_kernel(seg_ref, mine_ref, other_ref, r_ref, tr_ref, X, Rb, Wb):
    lane=lax.broadcasted_iota(jnp.int32,(8,128),1); row=lax.broadcasted_iota(jnp.int32,(8,128),0)
    grp=lane//32
    l32=lax.broadcasted_iota(jnp.int32,(32,256),1)
    r32=lax.broadcasted_iota(jnp.int32,(32,256),0)
    bd=(lax.broadcasted_iota(jnp.int32,(128,128),0)//32)==(lax.broadcasted_iota(jnp.int32,(128,128),1)//32)
    l256=lax.broadcasted_iota(jnp.int32,(128,256),1); r256=lax.broadcasted_iota(jnp.int32,(128,256),0)&31
    odd = (lax.axis_index("sub") % 2) == 1
    mine, other = mine_ref[...], other_ref[...]
    first = jnp.where(odd, other, mine)
    second = jnp.where(odd, mine[0], other[0])
    levels = [seg_ref[...], first[0], first[1], (first[1] + second) * 0.5]
    for t, packed in enumerate(levels):
        rows = unpack(packed)
        for kb in range(8):
            X[kb, 32 * t : 32 * t + 32, :] = rows[32 * kb : 32 * kb + 32, :]
    pending=[]
    def tick(step):
        if pending and step%2==2-1: pending.pop(0)()
    def update(i,L,ps,off):
        X[i]=jnp.where((l256>=off)&(l256<off+32),0.0,X[i])-mms(L,ps)
    def emit(kb,panel,Pf):
        off=32*kb; lo=off%128
        for t in range(4):
            pt=panel[32*t:32*t+32,:]
            sh=(lo-32*t)%128
            d=Pf
            if sh: d=pltpu.roll(d,sh,1)
            d2=jnp.concatenate([d,d],1)
            Rb[t,off:off+32,:]=jnp.where(l32>=off+32,pt,jnp.where((l32>=off)&(l32-off>=r32),d2,0.0))
            if t>0: Wb[t-1,off:off+32,:]=jnp.where(l32<off+32,pt,0.0)
    def place(rows_of, block, lo):
        out=[]
        for t in range(4):
            sh=(32*t-lo)%128
            v=rows_of(t)
            out.append(pltpu.roll(v,sh,1) if sh else v)
        return out
    grp32=lax.broadcasted_iota(jnp.int32,(32,128),1)//32
    state={}
    def placed(block, cb):
        off=32*cb; c0=off//128*128
        return place(lambda t:X[block,32*t:32*t+32,c0:c0+128],block,off%128)
    def pick(vs):
        acc=vs[0]
        for t in range(1,4): acc=jnp.where(grp32==t,vs[t],acc)
        return acc
    def prep(kb):
        state['d']=pick(placed(kb+1,kb+1))
        if kb+2<8:
            state['q2']=rstack(jnp.where(bd,jnp.concatenate(placed(kb,kb+2),0),0.0))
            state['qpre']=pick(placed(kb+1,kb+2))
    def rows(x): return [x[8*r:8*r+8,:] for r in range(4)]
    def make_panel(kb,Vf):
        off=32*kb
        Wbd=jnp.where(bd,jnp.concatenate([Vf]*4,0),0.0)
        x=X[kb]
        x=jnp.where((l256>=off)&(l256<off+32),jnp.where(l256-off==r256,1.0,0.0),x)
        state['panel']=mms(lstack(Wbd),rstack(x))
        state['ps']=rstack(state['panel'])
        state['ch']={}
    def go(i,off):
        c=i//4
        if c not in state['ch']: state['ch'][c]=jnp.transpose(state['panel'][:,c*128:c*128+128])
        T=state['ch'][c][(i%4)*32:(i%4)*32+32,:]
        update(i,lstack(jnp.where(bd,jnp.concatenate([T]*4,0),0.0)),state['ps'],off)
    def emit_out(kb,Pf): emit(kb,state['panel'],Pf)
    def first_quarter(t):
        tr_ref[t,0:128,0:128]=mmt(Rb[t,0:128,0:128],Wb[t,0:128,0:128]).astype(jnp.bfloat16)
        tr_ref[t,128:256,0:128]=jnp.zeros((128,128),jnp.bfloat16)
    p32=pick(placed(0,0)); q32=pick(placed(0,1))
    for kb in range(8):
        if kb==0: pending.append(functools.partial(prep,0))
        P,V,Q=eliminate(rows(p32),rows(q32) if kb<7 else None,lane,row,tick)
        while pending: pending.pop(0)()
        Pf=jnp.concatenate(P,0); Vf=jnp.concatenate(V,0)
        if kb<7:
            h,l=split(jnp.concatenate(Q,0))
            left=jnp.concatenate([h,h,l],0)
            G=dg(left,jnp.concatenate([h,l,h],0),((0,),(0,)))
            p32=state['d']-pick([G[32*t:32*t+32,:] for t in range(4)])
            if kb+2<8:
                h2,l2=split(mms(lstack(Vf),state['q2']))
                G2=dg(left,jnp.concatenate([h2,l2,h2],0),((0,),(0,)))
                q32=state['qpre']-pick([G2[32*t:32*t+32,:] for t in range(4)])
        pending.append(functools.partial(make_panel,kb,Vf))
        for i in range(kb+1,8):
            pending.append(functools.partial(go,i,32*kb))
            if i==min(kb+2,7) and kb+1<7: pending.append(functools.partial(prep,kb+1))
        pending.append(functools.partial(emit_out,kb,Pf))
        if kb==3:
            for t in range(3): pending.append(functools.partial(first_quarter,t))
    while pending: pending.pop(0)()
    r_ref[...]=Rb[0]
    for t in range(3):
        tr_ref[t,0:128,128:256]=mmt(Rb[t,0:128,:],Wb[t,128:256,:]).astype(jnp.bfloat16)
        tr_ref[t,128:256,128:256]=mmt(Rb[t,128:256,128:256],Wb[t,128:256,128:256]).astype(jnp.bfloat16)

def factor_all(seg_gram, mine, other):
    return pl.pallas_call(
        factor_kernel,
        out_shape=(
            jax.ShapeDtypeStruct((256, 256), jnp.float32),
            jax.ShapeDtypeStruct((LEVELS, 256, 256), jnp.bfloat16),
        ),
        in_specs=[VMEM] * 3,
        out_specs=[VMEM] * 2,
        scratch_shapes=[
            pltpu.VMEM((8, 128, 256), jnp.float32),
            pltpu.VMEM((4, 256, 256), jnp.float32),
            pltpu.VMEM((3, 256, 256), jnp.float32),
        ],
        compiler_params=params(),
    )(seg_gram, mine, other)


def body(
    near_blocks, sample_cols, near_list, row_basis_t, col_basis_t, couplings, far_source, far_dest
):
    leaf_count, near_count, leaf_rows, _ = near_blocks.shape
    width = sample_cols.shape[1]
    rank = row_basis_t.shape[1]
    n_seg, n_sub = lax.axis_size("seg"), lax.axis_size("sub")
    n = n_seg * n_sub
    rows = leaf_count * leaf_rows

    swap = lax.ppermute(sample_cols, AXES, [(i, i ^ 1) for i in range(n)])
    ahead = [(i, i + 1) for i in range(1, n - 1, 2)]
    cross = lax.ppermute(sample_cols, AXES, ahead + [(j, i) for i, j in ahead])

    slots = far_source.shape[3]
    basis_first, swap = lax.optimization_barrier((col_basis_t, swap))
    high = n_seg // PLANE
    hbm = pl.BlockSpec(memory_space=pltpu.HBM)
    bf16 = jnp.bfloat16
    mine, row_basis, *pays = pl.pallas_call(
        first_kernel,
        out_shape=[
            jax.ShapeDtypeStruct((1, leaf_count * rank + 8, width), bf16),
            jax.ShapeDtypeStruct(row_basis_t.shape, bf16),
        ]
        + [jax.ShapeDtypeStruct((1, high * rank + 8, slots * rank), bf16)] * PLANE,
        in_specs=[hbm] * 4 + [VMEM] * 2,
        out_specs=[VMEM] * (2 + PLANE),
        scratch_shapes=[
            pltpu.VMEM(col_basis_t.shape, bf16),
            pltpu.VMEM(sample_cols.shape, bf16),
            pltpu.VMEM(couplings.shape[2:], bf16),
            pltpu.VMEM((2, 8, 256), jnp.float32),
            pltpu.SemaphoreType.DMA((4,)),
        ],
        compiler_params=params(FIRST_KIB),
    )(
        basis_first,
        sample_cols,
        couplings,
        row_basis_t,
        jnp.swapaxes(far_source[0, 0], 0, 1),
        jnp.swapaxes(far_dest[0, 0], 0, 1),
    )

    column = [hop(mine, PLANE * k, PLANE * k) for k in range(1, high)]
    gathered = [hop(pays[m], m, m) for m in range(1, PLANE)]
    def near_leaf(leaf):
        return pl.pallas_call(
            functools.partial(near_kernel, leaf),
            out_shape=jax.ShapeDtypeStruct((leaf_rows, width), jnp.float32),
            in_specs=[hbm, VMEM, hbm, VMEM, VMEM],
            out_specs=VMEM,
            scratch_shapes=[
                pltpu.VMEM((3 * leaf_count + 1, leaf_rows, width), bf16),
                pltpu.SMEM(near_list.shape, jnp.int32),
                pltpu.SemaphoreType.DMA((1 + leaf_count,)),
            ],
            compiler_params=params(NEAR_KIB),
            cost_estimate=pl.CostEstimate(
                flops=2 * leaf_rows * near_count * leaf_rows * width,
                bytes_accessed=near_blocks.size + 5 * rows * width * 2,
                transcendentals=0,
            ),
        )(near_list, lax.slice_in_dim(near_blocks, leaf, leaf + 1, axis=0), sample_cols, swap, cross)

    near_parts = [near_leaf(0)]
    column, gathered, near_parts = lax.optimization_barrier((column, gathered, near_parts))
    own, *parts = pl.pallas_call(
        functools.partial(partial_kernel, leaf_count, slots),
        out_shape=[jax.ShapeDtypeStruct((1, leaf_count * rank, width), jnp.float32)]
        + [jax.ShapeDtypeStruct((1, leaf_count * rank, width), bf16)] * (PLANE - 1),
        in_specs=[VMEM] * (PLANE + high),
        out_specs=[VMEM] * PLANE,
        compiler_params=params(),
    )(mine, *column, pays[0], *gathered)
    got = [hop(parts[m - 1], m, m) for m in range(PLANE - 1, 0, -1)]

    near_parts = near_parts + [near_leaf(leaf) for leaf in range(1, leaf_count)]
    samples, gram = pl.pallas_call(
        combine_kernel,
        out_shape=(
            jax.ShapeDtypeStruct((rows, width), jnp.bfloat16),
            jax.ShapeDtypeStruct((320, 128), jnp.float32),
        ),
        in_specs=[VMEM] * (2 + leaf_count + PLANE - 1),
        out_specs=[VMEM] * 2,
        compiler_params=params(),
    )(row_basis, own, *near_parts, *got)

    total, mask = gram, 1
    while mask < n_sub:
        total = total + sub_hop(total, mask)
        mask *= 2
    seg_gram = total / (n_sub * rows)
    rounded = seg_gram.astype(jnp.bfloat16)
    near = [
        hop(rounded, *masks).astype(jnp.float32) for masks in ((1, 4), (2, 6), (3, 5), (None, 7))
    ]
    odd = (lax.axis_index("sub") % 2) == 1
    pair = seg_gram + near[0]
    quad = (near[1] + near[2]) + pair
    far_quad = (near[0] + near[1]) + (near[2] + near[3])
    sent = jnp.stack([jnp.where(odd, far_quad * 0.25, pair * 0.5), quad * 0.25])
    received = sub_hop(sent, 1)
    segment_factor, transfers = factor_all(seg_gram, sent, received)
    return (samples, segment_factor, transfers[None])


def solution(mesh):
    in_specs = (
        P(("seg", "sub"), None, None, None),
        P(("seg", "sub"), None),
        P(("seg", "sub"), None),
        P(("seg", "sub"), None, None),
        P(("seg", "sub"), None, None),
        P("seg", "sub", None, None, None),
        P("seg", "sub", None, None),
        P("seg", "sub", None, None),
    )
    out_specs = (P(("seg", "sub"), None), P("seg", None), P("seg", None, None, None))
    return jax.shard_map(body, mesh=mesh, in_specs=in_specs, out_specs=out_specs, check_vma=False)
```
